256 devices in a mesh: aux: 32 (over y, x, core), occ: 8 (over z).
Axes of the slice: x: 4, y: 4, z: 8, core: 2. Of those that a mesh axis runs over, the one named last changes fastest.
Arguments:
- integrals: bfloat16 [256, 8, 48, 4096], P(('aux', 'occ')), may hold values from -1 to 1
- mu_shells: int32 [256, 8], P(('aux', 'occ')), may hold values from 0 to 63
- nu_shells: int32 [256, 8], P(('aux', 'occ')), may hold values from 0 to 21
- block_count: int32 [256], P(('aux', 'occ')), may hold values from 1 to 8, as said below
- occ_coeffs: bfloat16 [4096, 32], replicated
- vir_coeffs: bfloat16 [1408, 1600], replicated, may hold values from -0.15625 to 0.15625
- occ_order: int32 [32], replicated, may hold values from 0 to 31, each once
- occ_energies: float32 [32], replicated, may hold values from -2 to -0.5
- vir_energies: float32 [1600], replicated, may hold values from 0.015 to 25
Outputs:
- amplitudes: bfloat16 [32, 1600, 1600], P('aux', 'occ')
- pair_energy: float32 [32], P('aux')
The draws below stay inside these ranges and needn't reach their ends.
Inputs may be any that keep to these rules, and one draw needn't show every extreme that they name: Only the first block_count[s] entries of slab s's block lists and integrals are screened in; some slab has all 8 slots in use.
All inputs are finite; a program needn't handle non-finite values.
Results may differ from the reference program's by a relative error of at most 0.017.
Values may be sent and summed in bfloat16 or wider, within the bound.
A program may use at most 128 MiB of HBM per device.

```python
import jax
import jax.numpy as jnp
from jax import lax

NAO = 4096
SHELL = 64
NU_W = 1408
NVIR = 1600
NBLK = 8
P_DEV = 48
OCC_W = 32
N_AUX = 32
N_OCC = 8
DEVICES = 256


def draw_block_count(key, part):
    key = jax.random.fold_in(key, 7)
    first, second = jax.random.split(key)
    counts = jax.random.randint(first, (DEVICES,), 1, NBLK + 1)
    fullest = jax.random.randint(second, (), 0, DEVICES)
    return jnp.where(jnp.arange(DEVICES) == fullest, NBLK, counts).astype(jnp.int32)


def draw_occ_coeffs(key, part):
    key = jax.random.fold_in(key, 11)
    first, second = jax.random.split(key)
    common = jax.random.normal(first, (NAO, 1), jnp.float32)
    single = jax.random.normal(second, (NAO, OCC_W), jnp.float32)
    values = (0.8 * common + 0.6 * single) / jnp.sqrt(jnp.float32(SHELL))
    return values.astype(jnp.bfloat16)


def rising_levels(key, base, growth):
    position = jnp.arange(NVIR, dtype=jnp.float32) / jnp.float32(NVIR)
    rough = jax.random.uniform(key, (NVIR,), jnp.float32, 0.8, 1.25)
    return base * jnp.exp(jnp.log(jnp.float32(growth)) * position) * rough


def draw_vir_energies(key, part):
    key = jax.random.fold_in(key, 13)
    values = rising_levels(key, 0.05, 300.0)
    return values.astype(jnp.float32)


def plant(values, stream_key, least, largest):
    dims = values.shape
    spot = [jax.random.randint(jax.random.fold_in(stream_key, axis), (), 0, dims[axis]) for axis in range(len(dims))]
    values = values.at[tuple(spot)].set(least)
    longest = dims.index(max(dims))
    spot[longest] = (spot[longest] + 1) % dims[longest]
    return values.at[tuple(spot)].set(largest)


def block_levels(own_key, extent, shards, low, top_value):
    gain = 1.0
    for dim, blocks in shards:
        heights = jax.random.uniform(jax.random.fold_in(jax.random.fold_in(own_key, 6), dim), (blocks,), jnp.float32, low / len(shards), top_value / len(shards))
        gain = gain * jnp.repeat(jnp.exp(heights), extent[dim] // blocks).reshape((-1,) + (1,) * (len(extent) - 1 - dim))
    return gain


def bell_draw(stream_key, dims, spread, limit, cuts=(), kind=jnp.bfloat16):
    factor_of = block_levels(stream_key, dims, cuts, -0.22, 0.18) if cuts else 1.0
    values = jax.random.normal(stream_key, dims, jnp.float32) * spread * factor_of
    return jnp.minimum(jnp.maximum(values, -limit), limit).astype(kind)


def setup_inputs(seed: int = 0) -> dict:
    splits = jax.random.split(jax.random.key(seed), 10)
    integrals = bell_draw(splits[0], (DEVICES, NBLK, P_DEV, SHELL * SHELL), 0.07, 1.0, ((0, 256),))
    mu_shells = plant(jax.random.randint(splits[1], (DEVICES, NBLK), 0, NAO // SHELL), jax.random.fold_in(splits[1], 1), 0, (NAO // SHELL) - 1).astype(jnp.int32)
    nu_shells = plant(jax.random.randint(splits[2], (DEVICES, NBLK), 0, NU_W // SHELL), jax.random.fold_in(splits[2], 1), 0, (NU_W // SHELL) - 1).astype(jnp.int32)
    block_count = draw_block_count(jax.random.fold_in(splits[9], 71), 0)
    occ_coeffs = draw_occ_coeffs(jax.random.fold_in(splits[9], 71), 0)
    vir_coeffs = bell_draw(splits[5], (NU_W, NVIR), NU_W ** -0.5, 0.15625)
    occ_order = jax.random.permutation(splits[6], OCC_W).astype(jnp.int32)
    occ_energies = jnp.clip(jax.random.uniform(splits[7], (OCC_W,), jnp.float32, -2.0, -0.5), -2.0, -0.5)
    vir_energies = draw_vir_energies(jax.random.fold_in(splits[9], 71), 0)
    return dict(integrals=integrals, mu_shells=mu_shells, nu_shells=nu_shells, block_count=block_count, occ_coeffs=occ_coeffs, vir_coeffs=vir_coeffs, occ_order=occ_order, occ_energies=occ_energies, vir_energies=vir_energies)


def reference(integrals, mu_shells, nu_shells, block_count, occ_coeffs, vir_coeffs, occ_order, occ_energies, vir_energies):
    occ_count = occ_order.shape[0]
    chosen = jnp.take(occ_coeffs, occ_order, axis=1)
    shell_rows = chosen.reshape(NAO // SHELL, SHELL, occ_count).astype(jnp.float32)
    shell_ids = jnp.arange(NU_W // SHELL, dtype=jnp.int32)
    slot_ids = jnp.arange(NBLK, dtype=jnp.int32)

    def one_slab(items):
        blocks, mus, nus, count = items
        rows = jnp.take(shell_rows, mus, axis=0)
        blocks = blocks.reshape(NBLK, P_DEV, SHELL, SHELL).astype(jnp.float32)
        parts = jnp.einsum("kpmn,kmi->kpin", blocks, rows)
        live = (slot_ids < count).astype(jnp.float32)
        place = (nus[:, None] == shell_ids[None, :]).astype(jnp.float32) * live[:, None]
        half = jnp.einsum("kpin,ks->pisn", parts, place).reshape(P_DEV, occ_count, NU_W).astype(jnp.bfloat16)
        rows_out = jnp.dot(half.reshape(P_DEV * occ_count, NU_W), vir_coeffs, preferred_element_type=jnp.float32)
        return rows_out.astype(jnp.bfloat16).reshape(P_DEV, occ_count, NVIR)

    ri_rows = lax.map(one_slab, (integrals, mu_shells, nu_shells, block_count))
    grouped = ri_rows.reshape(N_AUX, N_OCC, P_DEV, occ_count, NVIR)
    chosen_energy = jnp.take(occ_energies, occ_order)

    def one_pair(index):
        partner_index = (index - 1) % occ_count
        own = lax.dynamic_index_in_dim(grouped, index, axis=3, keepdims=False)
        other = lax.dynamic_index_in_dim(grouped, partner_index, axis=3, keepdims=False)
        own = jnp.swapaxes(own, 0, 1).reshape(N_OCC, N_AUX * P_DEV, NVIR)
        other = jnp.swapaxes(other, 0, 1).reshape(N_OCC, N_AUX * P_DEV, NVIR)

        def group_term(carry, pieces):
            own_group, other_group = pieces
            term = jnp.dot(other_group.T, own_group, preferred_element_type=jnp.float32)
            rounded = lax.optimization_barrier(term.astype(jnp.bfloat16))
            return carry + rounded.astype(jnp.float32), None

        start = jnp.zeros((NVIR, NVIR), jnp.float32)
        pair_integrals, unused = lax.scan(group_term, start, (own, other))
        e_pair = jnp.take(chosen_energy, index) + jnp.take(chosen_energy, partner_index)
        denominator = e_pair - vir_energies[:, None] - vir_energies[None, :]
        ratio = pair_integrals / denominator
        energy = jnp.sum(ratio * (2.0 * pair_integrals - pair_integrals.T)) / (NVIR * NVIR)
        return ratio.astype(jnp.bfloat16), energy

    amplitudes, pair_energy = lax.map(one_pair, jnp.arange(occ_count, dtype=jnp.int32))
    return amplitudes, pair_energy
```

```python
import functools

import jax
import jax.numpy as jnp
from jax import lax
from jax.experimental import pallas as pl
from jax.experimental.pallas import tpu as pltpu
from jax.sharding import PartitionSpec as P

SHELL = 64
LANE = 128
ROWS = 16
MESH = pl.DeviceIdType.MESH
F32 = jnp.float32
BF16 = jnp.bfloat16
NT = (((1,), (1,)), ((), ()))


def left_half(shape):
    return lax.broadcasted_iota(jnp.int32, shape, len(shape) - 1) < SHELL


def half_kernel(slots, occ_count, mu_ref, x_ref, occ_ref, order_ref, merge_ref, out_ref, tall, lhs, spread, prods):
    lane_tiles = SHELL * SHELL // LANE
    depth = slots * lane_tiles
    wide = slots * occ_count

    @pl.when(pl.program_id(0) == 0)
    def _():
        row = lax.broadcasted_iota(jnp.int32, (SHELL, SHELL), 0)
        col = lax.broadcasted_iota(jnp.int32, (SHELL, SHELL), 1)
        split = (col == 2 * (row % lane_tiles) + row // lane_tiles).astype(F32).astype(BF16)
        picked = lax.broadcasted_iota(jnp.int32, (occ_count, wide), 0) == order_ref[...]
        for k in range(slots):
            start = pl.multiple_of(mu_ref[k] * SHELL, SHELL)
            rows = occ_ref[pl.ds(start, SHELL), :]
            parted = jnp.dot(split, rows, preferred_element_type=F32).astype(BF16)
            picker = jnp.where(picked, merge_ref[k : k + 1, :], 0.0).astype(BF16)
            both = jnp.dot(parted, picker, preferred_element_type=F32)
            tall[k * lane_tiles : (k + 1) * lane_tiles, :] = both[:lane_tiles]
            tall[depth + k * lane_tiles : depth + (k + 1) * lane_tiles, :] = both[lane_tiles:]
        lhs[...] = tall[...].T.astype(BF16)

    @pl.loop(0, slots)
    def _(k):
        for t in range(lane_tiles):
            at = pl.multiple_of((k * lane_tiles + t) * ROWS, ROWS)
            spread[pl.ds(at, ROWS), :] = x_ref[k, :, t * LANE : (t + 1) * LANE].astype(F32)

    half_rows = ROWS // 2
    left = left_half((depth, LANE))
    for r in range(0, half_rows, 2):
        columns = []
        for e in range(2):
            one = spread[pl.ds(r + e, depth, stride=ROWS), :]
            two = spread[pl.ds(r + e + half_rows, depth, stride=ROWS), :]
            low = jnp.where(left, one, pltpu.roll(two, SHELL, 1))
            high = jnp.where(left, pltpu.roll(one, SHELL, 1), two)
            columns.append(jnp.concatenate([low, high], axis=0).astype(BF16))
        both = jnp.dot(lhs[...], jnp.concatenate(columns, axis=1), preferred_element_type=F32)
        for e in range(2):
            prods[(r + e) * wide : (r + e + 1) * wide, :] = both[:, e * LANE : (e + 1) * LANE]

    left = left_half((half_rows, LANE))
    for i in range(occ_count + 1):
        batch = (i - 1) % occ_count
        for q in range(slots // 2):
            one = prods[pl.ds(2 * q * occ_count + batch, half_rows, stride=wide), :]
            two = prods[pl.ds((2 * q + 1) * occ_count + batch, half_rows, stride=wide), :]
            top = jnp.where(left, one, pltpu.roll(two, SHELL, 1))
            low = jnp.where(left, pltpu.roll(one, SHELL, 1), two)
            out_ref[i, :, q * LANE : (q + 1) * LANE] = jnp.concatenate([top, low], axis=0).astype(BF16)


def half_rows_of(integrals, mu, merge, order, occ_coeffs):
    slots, slab, _ = integrals.shape
    nao, occ_count = occ_coeffs.shape
    wide = slots * occ_count
    depth = slots * SHELL * SHELL // LANE
    return pl.pallas_call(
        functools.partial(half_kernel, slots, occ_count),
        grid_spec=pltpu.PrefetchScalarGridSpec(
            num_scalar_prefetch=1,
            grid=(slab // ROWS,),
            in_specs=[
                pl.BlockSpec((slots, ROWS, SHELL * SHELL), lambda p, mu: (0, p, 0)),
                pl.BlockSpec((nao, occ_count), lambda p, mu: (0, 0)),
                pl.BlockSpec((1, wide), lambda p, mu: (0, 0)),
                pl.BlockSpec((slots, wide), lambda p, mu: (0, 0)),
            ],
            out_specs=pl.BlockSpec((occ_count + 1, ROWS, slots * SHELL), lambda p, mu: (0, p, 0)),
            scratch_shapes=[
                pltpu.VMEM((2 * depth, wide), F32),
                pltpu.VMEM((wide, 2 * depth), BF16),
                pltpu.VMEM((depth * ROWS, LANE), F32),
                pltpu.VMEM((ROWS // 2 * wide, LANE), F32),
            ],
        ),
        out_shape=jax.ShapeDtypeStruct((occ_count + 1, slab, slots * SHELL), BF16),
        compiler_params=pltpu.CompilerParams(vmem_limit_bytes=40 * 2**20),
    )(mu, integrals, occ_coeffs, order, merge)


def pair_kernel(
    n_aux,
    n_occ,
    ext_ref,
    meta_ref,
    vir_ref,
    erow_ref,
    eblock_ref,
    eocc_ref,
    order_ref,
    amp_ref,
    energy_ref,
    got,
    metas,
    places,
    tiles,
    half_y,
    half_x,
    vir,
    tall,
    vir_t,
    lhs,
    wide,
    own,
    out_ring,
    in_ring,
    out_tile,
    in_tile,
    ratios,
    part,
    parts,
    local_sem,
    pair_send,
    pair_recv,
    lone_send,
    lone_recv,
    meta_send,
    meta_recv,
    pass_send,
    pass_recv,
    ring_send,
    ring_recv,
    tile_send,
    tile_recv,
    part_send,
    part_recv,
):
    a = lax.axis_index("aux")
    g = lax.axis_index("occ")
    odd = lax.rem(a, 2)
    mate = a + 1 - 2 * odd
    steps = n_aux // 2
    nu_w, nvir = vir.shape
    width = nvir // n_occ
    padded = vir_t.shape[1]
    slab = got.shape[2]
    packs = got.shape[3] // LANE
    nu_tiles = nu_w // LANE

    def aux(step):
        return lax.rem(a + step + 2 * n_aux, n_aux)

    def occ(step):
        return lax.rem(g + step + 2 * n_occ, n_occ)

    barrier = pltpu.get_barrier_semaphore()

    @pl.loop(1, n_aux)
    def _(d):
        pl.semaphore_signal(barrier, inc=1, device_id={"aux": aux(d)}, device_id_type=MESH)

    @pl.loop(1, n_occ)
    def _(d):
        pl.semaphore_signal(barrier, inc=1, device_id={"occ": occ(d)}, device_id_type=MESH)

    load_vir = pltpu.make_async_copy(vir_ref, vir, local_sem.at[0])
    load_vir.start()
    keep = pltpu.make_async_copy(ext_ref.at[pl.ds(a, 2)], got.at[a], local_sem.at[1])
    keep.start()
    pl.semaphore_wait(barrier, n_aux + n_occ - 2)

    def meta_copy(d):
        return pltpu.make_async_remote_copy(
            meta_ref, metas.at[a], meta_send.at[d], meta_recv.at[d], device_id={"aux": aux(d)}, device_id_type=MESH
        )

    def pair_copy(d):
        to = aux(2 * d)
        return pltpu.make_async_remote_copy(
            ext_ref.at[pl.ds(to, 2)], got.at[a], pair_send.at[d], pair_recv.at[d], device_id={"aux": to}, device_id_type=MESH
        )

    def lone_copy(d):
        to = aux(2 * d + 1)
        side = 1 - odd
        return pltpu.make_async_remote_copy(
            ext_ref.at[to + side],
            got.at[a, side],
            lone_send.at[d],
            lone_recv.at[d],
            device_id={"aux": to},
            device_id_type=MESH,
        )

    def pass_copy(d):
        source = aux(-2 * d)
        return pltpu.make_async_remote_copy(
            got.at[source, 1 - odd],
            got.at[source, odd],
            pass_send.at[d],
            pass_recv.at[d],
            device_id={"aux": mate},
            device_id_type=MESH,
        )

    @pl.loop(1, n_aux)
    def _(d):
        meta_copy(d).start()

    lone_copy(0).start()

    @pl.loop(1, steps)
    def _(d):
        pair_copy(d).start()
        lone_copy(d).start()

    metas[a] = meta_ref[...]
    tiles[:, 2 * packs] = jnp.zeros((2, slab, LANE), BF16)

    load_vir.wait()
    for w in range(0, nvir, LANE):
        end = min(w + LANE, nvir)
        tall[w:end, :] = vir[:, w:end].astype(F32).T

    @pl.loop(0, n_occ)
    def _(c):
        rows = tall[pl.ds(pl.multiple_of(c * width, 8), width), :]
        if padded > width:
            rows = jnp.concatenate([rows, jnp.zeros((padded - width, nu_w), F32)], axis=0)
        vir_t[c] = rows.astype(BF16)

    @pl.loop(1, n_aux)
    def _(d):
        meta_copy(d).wait_recv()

    placing = pltpu.make_async_copy(metas, places, local_sem.at[2])
    placing.start()
    placing.wait()

    left = left_half((slab, LANE))

    def spread(source):
        for side in range(2):
            for q in range(packs):
                tile = got[source, side, :, q * LANE : (q + 1) * LANE]
                tiles[side, q] = tile
                tiles[side, packs + q] = pltpu.roll(tile.astype(F32), SHELL, 1).astype(BF16)
        rows = pl.ds(pl.multiple_of(source * slab, ROWS), slab)
        for c in range(nu_tiles):
            first = places[source, 0, 2 * c]
            second = places[source, 0, 2 * c + 1]
            columns = slice(c * LANE, (c + 1) * LANE)
            half_y[rows, columns] = jnp.where(left, tiles[0, first], tiles[0, second])
            half_x[rows, columns] = jnp.where(left, tiles[1, first], tiles[1, second])

    keep.wait()
    pass_copy(0).start()
    spread(a)

    @pl.loop(1, steps)
    def _(d):
        pair_copy(d).wait_recv()
        pass_copy(d).start()
        spread(aux(-2 * d))

    @pl.loop(0, steps)
    def _(d):
        lone_copy(d).wait_recv()
        pass_copy(lax.rem(d + 1 - odd, steps)).wait_recv()
        spread(aux(-2 * d - 1))

    cut = (padded // ROWS + 1) // 2 * ROWS
    spans = (slice(0, cut), slice(cut, padded))
    way = 1 - 2 * odd

    def ring_copy(t, side):
        return pltpu.make_async_remote_copy(
            out_ring.at[t, pl.ds(spans[side].start, spans[side].stop - spans[side].start)],
            in_ring.at[t, pl.ds(spans[side].start, spans[side].stop - spans[side].start)],
            ring_send.at[side, t],
            ring_recv.at[side, t],
            device_id={"occ": occ(way if side == 0 else -way)},
            device_id_type=MESH,
        )

    @pl.loop(0, n_occ)
    def _(t):
        lhs[spans[0], :] = vir_t[occ(-way * (t + 1)), spans[0], :]
        lhs[spans[1], :] = vir_t[occ(way * (t + 1)), spans[1], :]
        for p in range(0, n_aux * slab, 256):
            end = min(p + 256, n_aux * slab)
            wide[:, p:end] = lax.dot_general(lhs[...], half_y[p:end, :], NT, preferred_element_type=F32).astype(BF16)
        for c in range(0, nu_w, 256):
            end = min(c + 256, nu_w)
            own[:, c:end] = jnp.dot(wide[...], half_x[:, c:end], preferred_element_type=F32)
        for side in range(2):
            span = spans[side]

            @pl.when(t == 0)
            def _():
                out_ring[t, span, :] = own[span, :].astype(BF16)

            @pl.when(t > 0)
            def _():
                ring_copy(t - 1, side).wait_recv()
                out_ring[t, span, :] = (own[span, :] + in_ring[t - 1, span, :].astype(F32)).astype(BF16)

            @pl.when(t < n_occ - 1)
            def _():
                ring_copy(t, side).start()

    last = n_occ - 1
    farthest = n_occ // 2

    def tile_step(d):
        return way * (d if d % 2 == 1 else -d)

    def tile_copy(d):
        return pltpu.make_async_remote_copy(
            out_tile.at[d - 1],
            in_tile.at[d - 1],
            tile_send.at[d - 1],
            tile_recv.at[d - 1],
            device_id={"occ": occ(tile_step(d))},
            device_id_type=MESH,
        )

    for d in range(1, farthest + 1):
        out_tile[d - 1] = lax.dot_general(
            vir_t[occ(tile_step(d))], out_ring[last], NT, preferred_element_type=F32
        ).astype(BF16)
        tile_copy(d).start()

    e_pair = eocc_ref[order_ref[a]] + eocc_ref[order_ref[aux(-1)]]
    block_row = jnp.broadcast_to(eblock_ref[g], (8, eblock_ref.shape[2]))
    e_rows = e_pair - block_row.T[:padded, 0:1]

    total = jnp.zeros((8, LANE), F32)

    def folded(values):
        rows, cols = values.shape
        if cols % LANE:
            values = jnp.concatenate([values, jnp.zeros((rows, LANE - cols % LANE), F32)], axis=1)
        result = values[:, :LANE]
        for c in range(LANE, values.shape[1], LANE):
            result = result + values[:, c : c + LANE]
        return jnp.sum(result.reshape(rows // 8, 8, LANE), axis=0)

    for c in range(0, nvir, 256):
        end = min(c + 256, nvir)
        pair = jnp.dot(out_ring[last], vir[:, c:end], preferred_element_type=F32)
        ratio = pair / (e_rows - erow_ref[:, c:end])
        amp_ref[0, :, c:end] = ratio[:width].astype(BF16)
        total = total + folded(ratio * (2.0 * pair))

    def block_ratio(h):
        block = lax.dot_general(out_ring[last], vir_t[h], NT, preferred_element_type=F32)
        return block / (e_rows - eblock_ref[h][:, :padded])

    same = lax.dot_general(vir_t[g], out_ring[last], NT, preferred_element_type=F32)
    total = total - folded(block_ratio(g) * same)
    for d in range(1, farthest + 1):
        ratios[d - 1] = block_ratio(occ(-tile_step(d)))
    for d in range(1, farthest + 1):
        weight = 1.0 if 2 * d == n_occ else 2.0
        tile_copy(d).wait_recv()
        total = total - weight * folded(ratios[d - 1] * in_tile[d - 1].astype(F32))

    part[...] = total

    def part_copy(d):
        return pltpu.make_async_remote_copy(
            part, parts.at[d], part_send.at[d], part_recv.at[d], device_id={"occ": occ(d)}, device_id_type=MESH
        )

    for d in range(1, n_occ):
        part_copy(d).start()
    for d in range(1, n_occ):
        part_copy(d).wait_recv()
        total = total + parts[d]
    energy_ref[0] = jnp.sum(total) / (nvir * nvir)

    for d in range(1, n_occ):
        part_copy(d).wait_send()
    for d in range(1, farthest + 1):
        tile_copy(d).wait_send()

    @pl.loop(0, n_occ - 1)
    def _(t):
        ring_copy(t, 0).wait_send()
        ring_copy(t, 1).wait_send()

    @pl.loop(1, n_aux)
    def _(d):
        meta_copy(d).wait_send()

    lone_copy(0).wait_send()
    pass_copy(0).wait_send()

    @pl.loop(1, steps)
    def _(d):
        pair_copy(d).wait_send()
        lone_copy(d).wait_send()
        pass_copy(d).wait_send()


def pair_results(n_aux, n_occ, ext, meta, vir_coeffs, erow, eblock, occ_energies, occ_order):
    _, slab, packed = ext.shape
    nu_w, nvir = vir_coeffs.shape
    width = nvir // n_occ
    padded = -(-width // ROWS) * ROWS
    aux_rows = n_aux * slab
    farthest = n_occ // 2
    steps = n_aux // 2
    vmem = pl.BlockSpec(memory_space=pltpu.VMEM)
    smem = pl.BlockSpec(memory_space=pltpu.SMEM)
    anywhere = pl.BlockSpec(memory_space=pl.ANY)
    dma = pltpu.SemaphoreType.DMA
    macs = 2 * n_occ * padded * aux_rows * nu_w
    return pl.pallas_call(
        functools.partial(pair_kernel, n_aux, n_occ),
        in_specs=[anywhere, vmem, anywhere, vmem, vmem, smem, smem],
        out_specs=(vmem, smem),
        out_shape=(jax.ShapeDtypeStruct((1, width, nvir), BF16), jax.ShapeDtypeStruct((1,), F32)),
        scratch_shapes=[
            pltpu.VMEM((n_aux, 2, slab, packed), BF16),
            pltpu.VMEM((n_aux, 8, LANE), jnp.int32),
            pltpu.SMEM((n_aux, 8, LANE), jnp.int32),
            pltpu.VMEM((2, 2 * packed // LANE + 1, slab, LANE), BF16),
            pltpu.VMEM((aux_rows, nu_w), BF16),
            pltpu.VMEM((aux_rows, nu_w), BF16),
            pltpu.VMEM((nu_w, nvir), BF16),
            pltpu.VMEM((nvir, nu_w), F32),
            pltpu.VMEM((n_occ, padded, nu_w), BF16),
            pltpu.VMEM((padded, nu_w), BF16),
            pltpu.VMEM((padded, aux_rows), BF16),
            pltpu.VMEM((padded, nu_w), F32),
            pltpu.VMEM((n_occ, padded, nu_w), BF16),
            pltpu.VMEM((n_occ - 1, padded, nu_w), BF16),
            pltpu.VMEM((farthest, padded, padded), BF16),
            pltpu.VMEM((farthest, padded, padded), BF16),
            pltpu.VMEM((farthest, padded, padded), F32),
            pltpu.VMEM((8, LANE), F32),
            pltpu.VMEM((n_occ, 8, LANE), F32),
            dma((3,)),
            dma((steps,)),
            dma((steps,)),
            dma((steps,)),
            dma((steps,)),
            dma((n_aux,)),
            dma((n_aux,)),
            dma((steps,)),
            dma((steps,)),
            dma((2, n_occ - 1)),
            dma((2, n_occ - 1)),
            dma((farthest,)),
            dma((farthest,)),
            dma((n_occ,)),
            dma((n_occ,)),
        ],
        compiler_params=pltpu.CompilerParams(
            collective_id=0, has_side_effects=True, vmem_limit_bytes=60 * 2**20
        ),
        cost_estimate=pl.CostEstimate(flops=2 * macs, bytes_accessed=2 * nu_w * nvir, transcendentals=0),
    )(ext, meta, vir_coeffs, erow, eblock, occ_energies, occ_order)


def local(
    n_aux,
    n_occ,
    integrals,
    mu_shells,
    nu_shells,
    block_count,
    occ_coeffs,
    vir_coeffs,
    occ_order,
    occ_energies,
    vir_energies,
):
    nu_w, nvir = vir_coeffs.shape
    occ_count = occ_order.shape[0]
    slots = integrals.shape[1]
    width = nvir // n_occ
    padded = -(-width // LANE) * LANE
    nu = nu_shells[0]
    slot = jnp.arange(slots, dtype=jnp.int32)
    live = slot < block_count[0]
    alike = (nu[:, None] == nu[None, :]) & live[:, None] & live[None, :]
    first = live & ~jnp.any(alike & (slot[None, :] < slot[:, None]), axis=1)
    merge = jnp.repeat((alike & first[None, :]).astype(F32), occ_count, axis=1)
    order = jnp.tile(occ_order, slots)[None, :]
    shells = jnp.arange(LANE, dtype=jnp.int32)
    found = first[None, :] & (nu[None, :] == shells[:, None])
    place = jnp.where(slot[None, :] % 2 == shells[:, None] % 2, slot[None, :] // 2, slots // 2 + slot[None, :] // 2)
    place = jnp.min(jnp.where(found, place, slots), axis=1)
    meta = jnp.broadcast_to(place[None, :], (8, LANE))
    ext = half_rows_of(integrals[0], mu_shells[0], merge, order, occ_coeffs)
    eblock = jnp.pad(vir_energies.reshape(n_occ, 1, width), ((0, 0), (0, 0), (0, padded - width)), constant_values=1.0)
    return pair_results(n_aux, n_occ, ext, meta, vir_coeffs, vir_energies[None, :], eblock, occ_energies, occ_order)


def solution(mesh):
    placed = (
        P(("aux", "occ"), None, None, None),
        P(("aux", "occ"), None),
        P(("aux", "occ"), None),
        P(("aux", "occ")),
        P(),
        P(),
        P(),
        P(),
        P(),
    )
    return jax.shard_map(
        functools.partial(local, mesh.shape["aux"], mesh.shape["occ"]),
        mesh=mesh,
        in_specs=placed,
        out_specs=(P("aux", "occ", None), P("aux")),
        check_vma=False,
    )
```

```python
import functools

import jax
import jax.numpy as jnp
from jax import lax
from jax.experimental import pallas as pl
from jax.experimental.pallas import tpu as pltpu
from jax.sharding import PartitionSpec as P

SHELL = 64
LANE = 128
ROWS = 16
HALF = ROWS // 2
MESH = pl.DeviceIdType.MESH
F32 = jnp.float32
BF16 = jnp.bfloat16
I32 = jnp.int32
NT = (((1,), (1,)), ((), ()))


def left_half(shape):
    return lax.broadcasted_iota(I32, shape, len(shape) - 1) < SHELL


def iota(shape, dim):
    return lax.broadcasted_iota(I32, shape, dim)


def first_of_kind(slots, nu_ref, count):
    live = [k < count for k in range(slots)]
    first = []
    for k in range(slots):
        new = live[k]
        for j in range(k):
            new = new & (nu_ref[0, j] != nu_ref[0, k])
        first.append(new)
    return live, first


def build_mixer(slots, occ_count, mu_ref, nu_ref, order_ref, live, first, occ, tall, mixer):
    lane_tiles = SHELL * SHELL // LANE
    depth = slots * lane_tiles
    wide = slots * occ_count
    lane = iota((1, wide), 1)
    batch = lane % occ_count
    target = lane // occ_count
    order = jnp.zeros((1, wide), I32)
    for i in range(occ_count):
        order = jnp.where(batch == i, order_ref[i], order)
    shell = jnp.full((1, wide), -1, I32)
    for k in range(slots):
        shell = jnp.where(target == k, jnp.where(first[k], nu_ref[0, k], -1), shell)
    picked = iota((occ_count, wide), 0) == order
    row = iota((SHELL, LANE), 0)
    col = iota((SHELL, LANE), 1)
    wanted = 2 * (row % lane_tiles) + row // lane_tiles
    for k in range(slots):
        mu = mu_ref[0, k]
        rows = occ[:, :LANE]
        for t in range(1, occ.shape[1] // LANE):
            rows = jnp.where(mu // 2 == t, occ[:, t * LANE : (t + 1) * LANE], rows)
        split = (col == wanted + mu % 2 * SHELL).astype(F32).astype(BF16)
        parted = lax.dot_general(split, rows, NT, preferred_element_type=F32).astype(BF16)
        here = jnp.where(live[k], nu_ref[0, k], -2)
        picker = (picked & (shell == here)).astype(F32).astype(BF16)
        both = jnp.dot(parted, picker, preferred_element_type=F32)
        tall[k * lane_tiles : (k + 1) * lane_tiles, :] = both[:lane_tiles]
        tall[depth + k * lane_tiles : depth + (k + 1) * lane_tiles, :] = both[lane_tiles:]
    mixer[...] = tall[...].T.astype(BF16)


def place_table(slots, nu_ref, first):
    shell = iota((8, LANE), 1)
    place = jnp.full((8, LANE), slots, I32)
    for k in range(slots):
        here = jnp.where(first[k], nu_ref[0, k], -1)
        turned = jnp.where(shell % 2 == k % 2, k // 2, slots // 2 + k // 2)
        place = jnp.where(shell == here, turned, place)
    return place


def half_transform(slots, occ_count, q, blocks, mixer, spread, prods, ext):
    lane_tiles = SHELL * SHELL // LANE
    depth = slots * lane_tiles
    wide = slots * occ_count

    @pl.loop(0, slots)
    def _(k):
        for t in range(lane_tiles):
            at = pl.multiple_of((k * lane_tiles + t) * ROWS, ROWS)
            spread[pl.ds(at, ROWS), :] = blocks[q, k, :, t * LANE : (t + 1) * LANE].astype(F32)

    left = left_half((depth, LANE))
    for r in range(0, HALF, 2):
        columns = []
        for e in range(2):
            one = spread[pl.ds(r + e, depth, stride=ROWS), :]
            two = spread[pl.ds(r + e + HALF, depth, stride=ROWS), :]
            low = jnp.where(left, one, pltpu.roll(two, SHELL, 1))
            high = jnp.where(left, pltpu.roll(one, SHELL, 1), two)
            columns.append(jnp.concatenate([low, high], axis=0).astype(BF16))
        both = jnp.dot(mixer[...], jnp.concatenate(columns, axis=1), preferred_element_type=F32)
        for e in range(2):
            prods[(r + e) * wide : (r + e + 1) * wide, :] = both[:, e * LANE : (e + 1) * LANE]

    left = left_half((HALF, LANE))
    for i in range(occ_count + 1):
        batch = (i - 1) % occ_count
        for s in range(slots // 2):
            one = prods[pl.ds(2 * s * occ_count + batch, HALF, stride=wide), :]
            two = prods[pl.ds((2 * s + 1) * occ_count + batch, HALF, stride=wide), :]
            top = jnp.where(left, one, pltpu.roll(two, SHELL, 1))
            low = jnp.where(left, pltpu.roll(one, SHELL, 1), two)
            ext[q, i, :, s * LANE : (s + 1) * LANE] = jnp.concatenate([top, low], axis=0).astype(BF16)


def folded(values):
    rows, cols = values.shape
    if cols % LANE:
        values = jnp.concatenate([values, jnp.zeros((rows, LANE - cols % LANE), F32)], axis=1)
    result = values[:, :LANE]
    for c in range(LANE, values.shape[1], LANE):
        result = result + values[:, c : c + LANE]
    return jnp.sum(result.reshape(rows // 8, 8, LANE), axis=0)


def pair_kernel(
    n_aux,
    n_occ,
    pieces,
    integrals_ref,
    mu_ref,
    nu_ref,
    count_ref,
    occ_ref,
    vir_ref,
    order_ref,
    eocc_ref,
    evir_ref,
    amp_ref,
    energy_ref,
    blocks,
    occ,
    tall,
    mixer,
    spread,
    prods,
    ext,
    got,
    meta,
    metas,
    places,
    tiles,
    half_y,
    half_x,
    vir,
    vir_t,
    erow,
    eblock,
    lhs,
    wide,
    own,
    out_ring,
    in_ring,
    out_tile,
    in_tile,
    ratios,
    part,
    parts,
    local_sem,
    keep_sem,
    meta_send,
    meta_recv,
    data_send,
    data_recv,
    pass_send,
    pass_recv,
    ring_send,
    ring_recv,
    tile_send,
    tile_recv,
    part_send,
    part_recv,
):
    a = lax.axis_index("aux")
    g = lax.axis_index("occ")
    odd = lax.rem(a, 2)
    chip = a // 2
    mate = a + 1 - 2 * odd
    chips = n_aux // 2
    slots = blocks.shape[1]
    chunks = blocks.shape[0]
    occ_count = occ.shape[0]
    nvir, nu_w = vir.shape
    width = nvir // n_occ
    padded = vir_t.shape[1]
    slab = chunks * ROWS
    packs = slots // 2
    nu_tiles = nu_w // LANE

    def near(step):
        if chips != 16:
            return lax.rem(chip + step + chips, chips)
        return lax.rem(chip // 4 + step // 4, 4) * 4 + lax.rem(chip + step, 4)

    def back(step):
        if chips != 16:
            return lax.rem(chip - step + chips, chips)
        return lax.rem(chip // 4 - step // 4 + 4, 4) * 4 + lax.rem(chip % 4 - step % 4 + 4, 4)

    def around(step):
        return lax.rem(g + step + 2 * n_occ, n_occ)

    loads = [pltpu.make_async_copy(occ_ref, occ, local_sem.at[0])]
    for q in range(chunks):
        loads.append(
            pltpu.make_async_copy(integrals_ref.at[:, pl.ds(q * ROWS, ROWS)], blocks.at[q], local_sem.at[q + 1])
        )
    load_vir = pltpu.make_async_copy(vir_ref, vir, local_sem.at[chunks + 1])
    for load in loads:
        load.start()
    load_vir.start()

    barrier = pltpu.get_barrier_semaphore()

    @pl.loop(1, chips)
    def _(d):
        pl.semaphore_signal(barrier, inc=1, device_id={"aux": 2 * near(d) + odd}, device_id_type=MESH)

    pl.semaphore_signal(barrier, inc=1, device_id={"aux": mate}, device_id_type=MESH)

    @pl.loop(1, n_occ)
    def _(d):
        pl.semaphore_signal(barrier, inc=1, device_id={"occ": around(d)}, device_id_type=MESH)

    live, first = first_of_kind(slots, nu_ref, count_ref[0])
    meta[...] = place_table(slots, nu_ref, first)
    metas[odd, chip] = meta[...]
    loads[0].wait()
    build_mixer(slots, occ_count, mu_ref, nu_ref, order_ref, live, first, occ, tall, mixer)

    def meta_copy(d):
        return pltpu.make_async_remote_copy(
            meta,
            metas.at[odd, chip],
            meta_send.at[d],
            meta_recv.at[d],
            device_id={"aux": 2 * near(d) + odd},
            device_id_type=MESH,
        )

    def meta_pass():
        return pltpu.make_async_remote_copy(
            metas.at[odd], metas.at[odd], meta_send.at[0], meta_recv.at[0], device_id={"aux": mate}, device_id_type=MESH
        )

    def data_copy(q, d):
        to = near(d)
        return pltpu.make_async_remote_copy(
            ext.at[q, pl.ds(2 * to, 3)],
            got.at[odd, chip, q],
            data_send.at[q, d],
            data_recv.at[q, d],
            device_id={"aux": 2 * to + odd},
            device_id_type=MESH,
        )

    def keep_copy(q):
        return pltpu.make_async_copy(ext.at[q, pl.ds(2 * chip, 3)], got.at[odd, chip, q], keep_sem.at[q])

    def pass_copy(q, d):
        view = got.at[odd, back(d), q, pl.ds(1 - odd, 2)]
        return pltpu.make_async_remote_copy(
            view, view, pass_send.at[q, d], pass_recv.at[q, d], device_id={"aux": mate}, device_id_type=MESH
        )

    pl.semaphore_wait(barrier, chips + n_occ - 1)

    @pl.loop(1, chips)
    def _(d):
        meta_copy(d).start()

    @pl.loop(0, chunks)
    def _(q):
        pltpu.make_async_copy(
            integrals_ref.at[:, pl.ds(pl.multiple_of(q * ROWS, ROWS), ROWS)], blocks.at[q], local_sem.at[q + 1]
        ).wait()
        half_transform(slots, occ_count, q, blocks, mixer, spread, prods, ext)
        keep_copy(q).start()

        @pl.loop(1, chips)
        def _(d):
            data_copy(q, d).start()

    tiles[:, 2 * packs] = jnp.zeros((2, slab, LANE), BF16)
    load_vir.wait()
    for c in range(n_occ):
        low = c * width // ROWS * ROWS
        high = -(-(c + 1) * width // ROWS) * ROWS
        off = c * width - low
        for w in range(0, nu_w, LANE):
            rows = vir[low:high, w : w + LANE].astype(F32)[off : off + width]
            if padded > width:
                rows = jnp.concatenate([rows, jnp.zeros((padded - width, LANE), F32)], axis=0)
            vir_t[c, :, w : w + LANE] = rows.astype(BF16)
    erow[...] = evir_ref[...].reshape(1, nvir)
    for c in range(n_occ):
        eblock[c] = jnp.concatenate(
            [erow[:, c * width : (c + 1) * width], jnp.ones((1, eblock.shape[2] - width), F32)], axis=1
        )

    @pl.loop(1, chips)
    def _(d):
        meta_copy(d).wait_recv()

    meta_pass().start()
    meta_pass().wait_recv()
    placing = pltpu.make_async_copy(metas, places, local_sem.at[chunks + 2])
    placing.start()

    for q in range(chunks):
        keep_copy(q).wait()
        pass_copy(q, 0).start()
    placing.wait()

    left = left_half((slab, LANE))

    def spread_out(parity, source):
        for side in range(2):
            for s in range(packs):
                tile = got[parity, source, :, odd + side, :, s * LANE : (s + 1) * LANE].reshape(slab, LANE)
                tiles[side, s] = tile
                tiles[side, packs + s] = pltpu.roll(tile.astype(F32), SHELL, 1).astype(BF16)
        rows = pl.ds(pl.multiple_of((parity * chips + source) * slab, ROWS), slab)
        for c in range(nu_tiles):
            one = places[parity, source, 0, 2 * c]
            two = places[parity, source, 0, 2 * c + 1]
            columns = slice(c * LANE, (c + 1) * LANE)
            half_y[rows, columns] = jnp.where(left, tiles[0, one], tiles[0, two])
            half_x[rows, columns] = jnp.where(left, tiles[1, one], tiles[1, two])

    spread_out(odd, chip)

    @pl.loop(0, chunks)
    def _(q):
        @pl.loop(1, chips)
        def _(d):
            data_copy(q, d).wait_recv()
            pass_copy(q, d).start()

            @pl.when(q == chunks - 1)
            def _():
                spread_out(odd, back(d))

    @pl.loop(0, chips)
    def _(d):
        @pl.loop(0, chunks)
        def _(q):
            pass_copy(q, d).wait_recv()

        spread_out(1 - odd, back(d))

    way = 1 - 2 * odd

    def ring_copy(t, k):
        row, rows, sign = pieces[k]
        return pltpu.make_async_remote_copy(
            out_ring.at[t, pl.ds(row, rows)],
            in_ring.at[t, pl.ds(row, rows)],
            ring_send.at[k, t],
            ring_recv.at[k, t],
            device_id={"occ": around(way * sign)},
            device_id_type=MESH,
        )

    @pl.loop(0, n_occ)
    def _(t):
        for row, rows, sign in pieces:
            lhs[row : row + rows, :] = vir_t[around(-sign * way * (t + 1)), row : row + rows, :]
        for p in range(0, n_aux * slab, 256):
            end = min(p + 256, n_aux * slab)
            wide[:, p:end] = lax.dot_general(lhs[...], half_y[p:end, :], NT, preferred_element_type=F32).astype(BF16)
        for c in range(0, nu_w, 256):
            end = min(c + 256, nu_w)
            own[:, c:end] = jnp.dot(wide[...], half_x[:, c:end], preferred_element_type=F32)
        for k, (row, rows, sign) in enumerate(pieces):
            span = slice(row, row + rows)

            @pl.when(t == 0)
            def _():
                out_ring[t, span, :] = own[span, :].astype(BF16)

            @pl.when(t > 0)
            def _():
                ring_copy(t - 1, k).wait_recv()
                out_ring[t, span, :] = (own[span, :] + in_ring[t - 1, span, :].astype(F32)).astype(BF16)

            @pl.when(t < n_occ - 1)
            def _():
                ring_copy(t, k).start()

    last = n_occ - 1
    farthest = n_occ // 2

    def tile_step(d):
        return way * (d if d % 2 == 1 else -d)

    def tile_copy(d):
        return pltpu.make_async_remote_copy(
            out_tile.at[d - 1],
            in_tile.at[d - 1],
            tile_send.at[d - 1],
            tile_recv.at[d - 1],
            device_id={"occ": around(tile_step(d))},
            device_id_type=MESH,
        )

    for d in range(farthest, 0, -1):
        out_tile[d - 1] = lax.dot_general(
            vir_t[around(tile_step(d))], out_ring[last], NT, preferred_element_type=F32
        ).astype(BF16)
        tile_copy(d).start()

    e_pair = eocc_ref[order_ref[a]] + eocc_ref[order_ref[lax.rem(a + n_aux - 1, n_aux)]]
    block_row = jnp.broadcast_to(eblock[g], (8, eblock.shape[2]))
    e_rows = e_pair - block_row.T[:padded, 0:1]

    total = jnp.zeros((8, LANE), F32)
    for c in range(0, nvir, 256):
        end = min(c + 256, nvir)
        pair = lax.dot_general(out_ring[last], vir[c:end, :], NT, preferred_element_type=F32)
        ratio = pair / (e_rows - erow[:, c:end])
        amp_ref[0, :, c:end] = ratio[:width].astype(BF16)
        total = total + folded(ratio * (2.0 * pair))

    def block_ratio(h):
        block = lax.dot_general(out_ring[last], vir_t[h], NT, preferred_element_type=F32)
        return block / (e_rows - eblock[h][:, :padded])

    same = lax.dot_general(vir_t[g], out_ring[last], NT, preferred_element_type=F32)
    total = total - folded(block_ratio(g) * same)
    for d in range(1, farthest + 1):
        ratios[d - 1] = block_ratio(around(-tile_step(d)))
    for d in range(1, farthest + 1):
        weight = 1.0 if 2 * d == n_occ else 2.0
        tile_copy(d).wait_recv()
        total = total - weight * folded(ratios[d - 1] * in_tile[d - 1].astype(F32))

    part[...] = total

    def part_copy(d):
        return pltpu.make_async_remote_copy(
            part, parts.at[d], part_send.at[d], part_recv.at[d], device_id={"occ": around(d)}, device_id_type=MESH
        )

    for d in range(1, n_occ):
        part_copy(d).start()
    for d in range(1, n_occ):
        part_copy(d).wait_recv()
        total = total + parts[d]
    energy_ref[0] = jnp.sum(total) / (nvir * nvir)

    for d in range(1, n_occ):
        part_copy(d).wait_send()
    for d in range(1, farthest + 1):
        tile_copy(d).wait_send()

    @pl.loop(0, n_occ - 1)
    def _(t):
        for k in range(len(pieces)):
            ring_copy(t, k).wait_send()

    meta_pass().wait_send()

    @pl.loop(1, chips)
    def _(d):
        meta_copy(d).wait_send()

    @pl.loop(0, chunks)
    def _(q):
        pass_copy(q, 0).wait_send()

        @pl.loop(1, chips)
        def _(d):
            data_copy(q, d).wait_send()
            pass_copy(q, d).wait_send()


def pair_results(
    n_aux, n_occ, integrals, mu_shells, nu_shells, block_count, occ_t, vir_t, occ_order, occ_energies, vir_energies
):
    slots, slab, _ = integrals.shape
    occ_count, nao = occ_t.shape
    nvir, nu_w = vir_t.shape
    width = nvir // n_occ
    padded = -(-width // ROWS) * ROWS
    chunks = slab // ROWS
    chips = n_aux // 2
    aux_rows = n_aux * slab
    farthest = n_occ // 2
    spread_rows = slots * SHELL * SHELL // LANE * ROWS
    mixed = slots * occ_count
    cuts = [padded * k // (4 * ROWS) * ROWS for k in range(5)]
    spans = [(low, high - low, sign) for low, high, sign in zip(cuts[:-1], cuts[1:], (1, 1, -1, -1))]
    pieces = [spans[k] for k in (0, 2, 1, 3) if spans[k][1]]
    vmem = pl.BlockSpec(memory_space=pltpu.VMEM)
    smem = pl.BlockSpec(memory_space=pltpu.SMEM)
    anywhere = pl.BlockSpec(memory_space=pl.ANY)
    dma = pltpu.SemaphoreType.DMA
    macs = 2 * n_occ * padded * aux_rows * nu_w
    return pl.pallas_call(
        functools.partial(pair_kernel, n_aux, n_occ, pieces),
        in_specs=[anywhere, smem, smem, smem, anywhere, anywhere, smem, smem, vmem],
        out_specs=(vmem, smem),
        out_shape=(jax.ShapeDtypeStruct((1, width, nvir), BF16), jax.ShapeDtypeStruct((1,), F32)),
        scratch_shapes=[
            pltpu.VMEM((chunks, slots, ROWS, SHELL * SHELL), BF16),
            pltpu.VMEM((occ_count, nao), BF16),
            pltpu.VMEM((slots * SHELL, mixed), F32),
            pltpu.VMEM((mixed, slots * SHELL), BF16),
            pltpu.VMEM((spread_rows, LANE), F32),
            pltpu.VMEM((HALF * mixed, LANE), F32),
            pltpu.VMEM((chunks, occ_count + 1, ROWS, slots * SHELL), BF16),
            pltpu.VMEM((2, chips, chunks, 3, ROWS, slots * SHELL), BF16),
            pltpu.VMEM((8, LANE), I32),
            pltpu.VMEM((2, chips, 8, LANE), I32),
            pltpu.SMEM((2, chips, 8, LANE), I32),
            pltpu.VMEM((2, slots + 1, slab, LANE), BF16),
            pltpu.VMEM((aux_rows, nu_w), BF16),
            pltpu.VMEM((aux_rows, nu_w), BF16),
            pltpu.VMEM((nvir, nu_w), BF16),
            pltpu.VMEM((n_occ, padded, nu_w), BF16),
            pltpu.VMEM((1, nvir), F32),
            pltpu.VMEM((n_occ, 1, -(-padded // LANE) * LANE), F32),
            pltpu.VMEM((padded, nu_w), BF16),
            pltpu.VMEM((padded, aux_rows), BF16),
            pltpu.VMEM((padded, nu_w), F32),
            pltpu.VMEM((n_occ, padded, nu_w), BF16),
            pltpu.VMEM((n_occ - 1, padded, nu_w), BF16),
            pltpu.VMEM((farthest, padded, padded), BF16),
            pltpu.VMEM((farthest, padded, padded), BF16),
            pltpu.VMEM((farthest, padded, padded), F32),
            pltpu.VMEM((8, LANE), F32),
            pltpu.VMEM((n_occ, 8, LANE), F32),
            dma((chunks + 3,)),
            dma((chunks,)),
            dma((chips,)),
            dma((chips,)),
            dma((chunks, chips)),
            dma((chunks, chips)),
            dma((chunks, chips)),
            dma((chunks, chips)),
            dma((len(pieces), n_occ - 1)),
            dma((len(pieces), n_occ - 1)),
            dma((farthest,)),
            dma((farthest,)),
            dma((n_occ,)),
            dma((n_occ,)),
        ],
        compiler_params=pltpu.CompilerParams(
            collective_id=0, has_side_effects=True, vmem_limit_bytes=60 * 2**20
        ),
        cost_estimate=pl.CostEstimate(flops=2 * macs, bytes_accessed=2 * nu_w * nvir, transcendentals=0),
    )(integrals, mu_shells, nu_shells, block_count, occ_t, vir_t, occ_order, occ_energies, vir_energies)


def local(
    n_aux,
    n_occ,
    integrals,
    mu_shells,
    nu_shells,
    block_count,
    occ_coeffs,
    vir_coeffs,
    occ_order,
    occ_energies,
    vir_energies,
):
    return pair_results(
        n_aux,
        n_occ,
        integrals[0],
        mu_shells,
        nu_shells,
        block_count,
        occ_coeffs.T,
        vir_coeffs.T,
        occ_order,
        occ_energies,
        vir_energies,
    )


def solution(mesh):
    placed = (
        P(("aux", "occ"), None, None, None),
        P(("aux", "occ"), None),
        P(("aux", "occ"), None),
        P(("aux", "occ")),
        P(),
        P(),
        P(),
        P(),
        P(),
    )
    return jax.shard_map(
        functools.partial(local, mesh.shape["aux"], mesh.shape["occ"]),
        mesh=mesh,
        in_specs=placed,
        out_specs=(P("aux", "occ", None), P("aux")),
        check_vma=False,
    )
```

```python
import functools

import jax
import jax.numpy as jnp
from jax import lax
from jax.experimental import pallas as pl
from jax.experimental.pallas import tpu as pltpu
from jax.sharding import PartitionSpec as P

SHELL = 64
LANE = 128
ROWS = 16
HALF = ROWS // 2
MESH = pl.DeviceIdType.MESH
F32 = jnp.float32
BF16 = jnp.bfloat16
I32 = jnp.int32
NT = (((1,), (1,)), ((), ()))


def left_half(shape):
    return lax.broadcasted_iota(I32, shape, len(shape) - 1) < SHELL


def iota(shape, dim):
    return lax.broadcasted_iota(I32, shape, dim)


def halves_apart(one, two, left):
    turned = pltpu.roll(jnp.where(left, two, one), SHELL, 1)
    return [jnp.where(left, one, turned), jnp.where(left, turned, two)]


def first_of_kind(slots, nu_ref, count):
    live = [k < count for k in range(slots)]
    first = []
    for k in range(slots):
        new = live[k]
        for j in range(k):
            new = new & (nu_ref[0, j] != nu_ref[0, k])
        first.append(new)
    return live, first


def build_mixer(slots, occ_count, mu_ref, nu_ref, order_ref, live, first, occ, tall, mixer):
    lane_tiles = SHELL * SHELL // LANE
    depth = slots * lane_tiles
    wide = slots * occ_count
    lane = iota((1, wide), 1)
    batch = lane % occ_count
    target = lane // occ_count
    order = jnp.zeros((1, wide), I32)
    for i in range(occ_count):
        order = jnp.where(batch == i, order_ref[i], order)
    shell = jnp.full((1, wide), -1, I32)
    for k in range(slots):
        shell = jnp.where(target == k, jnp.where(first[k], nu_ref[0, k], -1), shell)
    picked = iota((occ_count, wide), 0) == order
    row = iota((SHELL, LANE), 0)
    col = iota((SHELL, LANE), 1)
    wanted = 2 * (row % lane_tiles) + row // lane_tiles
    for k in range(slots):
        mu = mu_ref[0, k]
        rows = occ[:, :LANE]
        for t in range(1, occ.shape[1] // LANE):
            rows = jnp.where(mu // 2 == t, occ[:, t * LANE : (t + 1) * LANE], rows)
        split = (col == wanted + mu % 2 * SHELL).astype(F32).astype(BF16)
        parted = lax.dot_general(split, rows, NT, preferred_element_type=F32).astype(BF16)
        here = jnp.where(live[k], nu_ref[0, k], -2)
        picker = (picked & (shell == here)).astype(F32).astype(BF16)
        both = jnp.dot(parted, picker, preferred_element_type=F32)
        tall[k * lane_tiles : (k + 1) * lane_tiles, :] = both[:lane_tiles]
        tall[depth + k * lane_tiles : depth + (k + 1) * lane_tiles, :] = both[lane_tiles:]
    mixer[...] = tall[...].T.astype(BF16)


def place_table(slots, nu_ref, first):
    shell = iota((8, LANE), 1)
    place = jnp.full((8, LANE), slots, I32)
    for k in range(slots):
        here = jnp.where(first[k], nu_ref[0, k], -1)
        turned = jnp.where(shell % 2 == k % 2, k // 2, slots // 2 + k // 2)
        place = jnp.where(shell == here, turned, place)
    return place


def half_transform(slots, occ_count, q, blocks, mixer, spread, prods, ext):
    lane_tiles = SHELL * SHELL // LANE
    depth = slots * lane_tiles
    wide = slots * occ_count

    @pl.loop(0, slots)
    def _(k):
        for t in range(lane_tiles):
            at = pl.multiple_of((k * lane_tiles + t) * ROWS, ROWS)
            spread[pl.ds(at, ROWS), :] = blocks[q, k, :, t * LANE : (t + 1) * LANE].astype(F32)

    left = left_half((depth, LANE))
    for r in range(0, HALF, 2):
        columns = []
        for e in range(2):
            one = spread[pl.ds(r + e, depth, stride=ROWS), :]
            two = spread[pl.ds(r + e + HALF, depth, stride=ROWS), :]
            columns.append(jnp.concatenate(halves_apart(one, two, left), axis=0).astype(BF16))
        both = jnp.dot(mixer[...], jnp.concatenate(columns, axis=1), preferred_element_type=F32)
        for e in range(2):
            prods[(r + e) * wide : (r + e + 1) * wide, :] = both[:, e * LANE : (e + 1) * LANE]

    left = left_half((HALF, LANE))
    for i in range(occ_count + 1):
        batch = (i - 1) % occ_count
        for s in range(slots // 2):
            one = prods[pl.ds(2 * s * occ_count + batch, HALF, stride=wide), :]
            two = prods[pl.ds((2 * s + 1) * occ_count + batch, HALF, stride=wide), :]
            pair = jnp.concatenate(halves_apart(one, two, left), axis=0)
            ext[q, i, :, s * LANE : (s + 1) * LANE] = pair.astype(BF16)


def folded(values):
    rows, cols = values.shape
    if cols % LANE:
        values = jnp.concatenate([values, jnp.zeros((rows, LANE - cols % LANE), F32)], axis=1)
    result = values[:, :LANE]
    for c in range(LANE, values.shape[1], LANE):
        result = result + values[:, c : c + LANE]
    return jnp.sum(result.reshape(rows // 8, 8, LANE), axis=0)


def pair_kernel(
    n_aux,
    n_occ,
    pieces,
    integrals_ref,
    mu_ref,
    nu_ref,
    count_ref,
    occ_ref,
    vir_ref,
    order_ref,
    eocc_ref,
    evir_ref,
    amp_ref,
    energy_ref,
    blocks,
    occ,
    tall,
    mixer,
    spread,
    prods,
    ext,
    got,
    meta,
    metas,
    places,
    tiles,
    half_y,
    half_x,
    vir,
    vir_t,
    erow,
    eblock,
    lhs,
    wide,
    own,
    out_ring,
    in_ring,
    out_rest,
    in_rest,
    total_u,
    out_lead,
    in_lead,
    out_tail,
    in_tail,
    ratio_lead,
    ratio_tail,
    part,
    parts,
    local_sem,
    keep_sem,
    meta_send,
    meta_recv,
    data_send,
    data_recv,
    pass_send,
    pass_recv,
    ring_send,
    ring_recv,
    lead_send,
    lead_recv,
    tail_send,
    tail_recv,
    part_send,
    part_recv,
):
    a = lax.axis_index("aux")
    g = lax.axis_index("occ")
    odd = lax.rem(a, 2)
    chip = a // 2
    mate = a + 1 - 2 * odd
    chips = n_aux // 2
    slots = blocks.shape[1]
    chunks = blocks.shape[0]
    occ_count = occ.shape[0]
    nvir, nu_w = vir.shape
    width = nvir // n_occ
    padded = vir_t.shape[1]
    slab = chunks * ROWS
    packs = slots // 2
    nu_tiles = nu_w // LANE

    def near(step):
        if chips != 16:
            return lax.rem(chip + step + chips, chips)
        return lax.rem(chip // 4 + step // 4, 4) * 4 + lax.rem(chip + step, 4)

    def back(step):
        if chips != 16:
            return lax.rem(chip - step + chips, chips)
        return lax.rem(chip // 4 - step // 4 + 4, 4) * 4 + lax.rem(chip % 4 - step % 4 + 4, 4)

    def around(step):
        return lax.rem(g + step + 2 * n_occ, n_occ)

    loads = [pltpu.make_async_copy(occ_ref, occ, local_sem.at[0])]
    for q in range(chunks):
        loads.append(
            pltpu.make_async_copy(integrals_ref.at[:, pl.ds(q * ROWS, ROWS)], blocks.at[q], local_sem.at[q + 1])
        )
    load_vir = pltpu.make_async_copy(vir_ref, vir, local_sem.at[chunks + 1])
    for load in loads:
        load.start()
    load_vir.start()

    barrier = pltpu.get_barrier_semaphore()

    @pl.loop(1, chips)
    def _(d):
        pl.semaphore_signal(barrier, inc=1, device_id={"aux": 2 * near(d) + odd}, device_id_type=MESH)

    pl.semaphore_signal(barrier, inc=1, device_id={"aux": mate}, device_id_type=MESH)

    @pl.loop(1, n_occ)
    def _(d):
        pl.semaphore_signal(barrier, inc=1, device_id={"occ": around(d)}, device_id_type=MESH)

    live, first = first_of_kind(slots, nu_ref, count_ref[0])
    meta[...] = place_table(slots, nu_ref, first)
    metas[odd, chip] = meta[...]
    loads[0].wait()
    build_mixer(slots, occ_count, mu_ref, nu_ref, order_ref, live, first, occ, tall, mixer)

    def meta_copy(d):
        return pltpu.make_async_remote_copy(
            meta,
            metas.at[odd, chip],
            meta_send.at[d],
            meta_recv.at[d],
            device_id={"aux": 2 * near(d) + odd},
            device_id_type=MESH,
        )

    def meta_pass():
        return pltpu.make_async_remote_copy(
            metas.at[odd], metas.at[odd], meta_send.at[0], meta_recv.at[0], device_id={"aux": mate}, device_id_type=MESH
        )

    def data_copy(q, d):
        to = near(d)
        return pltpu.make_async_remote_copy(
            ext.at[q, pl.ds(2 * to, 3)],
            got.at[odd, chip, q],
            data_send.at[q, d],
            data_recv.at[q, d],
            device_id={"aux": 2 * to + odd},
            device_id_type=MESH,
        )

    def keep_copy(q):
        return pltpu.make_async_copy(ext.at[q, pl.ds(2 * chip, 3)], got.at[odd, chip, q], keep_sem.at[q])

    def pass_copy(q, d):
        view = got.at[odd, back(d), q, pl.ds(1 - odd, 2)]
        return pltpu.make_async_remote_copy(
            view, view, pass_send.at[q, d], pass_recv.at[q, d], device_id={"aux": mate}, device_id_type=MESH
        )

    pl.semaphore_wait(barrier, chips + n_occ - 1)

    @pl.loop(1, chips)
    def _(d):
        meta_copy(d).start()

    @pl.loop(0, chunks)
    def _(q):
        pltpu.make_async_copy(
            integrals_ref.at[:, pl.ds(pl.multiple_of(q * ROWS, ROWS), ROWS)], blocks.at[q], local_sem.at[q + 1]
        ).wait()
        half_transform(slots, occ_count, q, blocks, mixer, spread, prods, ext)
        keep_copy(q).start()

        @pl.loop(1, chips)
        def _(d):
            data_copy(q, d).start()

    tiles[:, 2 * packs] = jnp.zeros((2, ROWS, LANE), BF16)
    load_vir.wait()
    for c in range(n_occ):
        low = c * width // ROWS * ROWS
        high = -(-(c + 1) * width // ROWS) * ROWS
        off = c * width - low
        for w in range(0, nu_w, LANE):
            rows = vir[low:high, w : w + LANE].astype(F32)[off : off + width]
            if padded > width:
                rows = jnp.concatenate([rows, jnp.zeros((padded - width, LANE), F32)], axis=0)
            vir_t[c, :, w : w + LANE] = rows.astype(BF16)
    erow[...] = evir_ref[...].reshape(1, nvir)
    for c in range(n_occ):
        eblock[c] = jnp.concatenate(
            [erow[:, c * width : (c + 1) * width], jnp.ones((1, eblock.shape[2] - width), F32)], axis=1
        )

    @pl.loop(1, chips)
    def _(d):
        meta_copy(d).wait_recv()

    meta_pass().start()
    meta_pass().wait_recv()
    placing = pltpu.make_async_copy(metas, places, local_sem.at[chunks + 2])
    placing.start()

    for q in range(chunks):
        keep_copy(q).wait()
        pass_copy(q, 0).start()
    placing.wait()

    left = left_half((ROWS, LANE))
    batch_rows = n_aux * ROWS

    def spread_out(q, parity, source):
        for side in range(2):
            for s in range(packs):
                tile = got[parity, source, q, odd + side, :, s * LANE : (s + 1) * LANE]
                tiles[side, s] = tile
                tiles[side, packs + s] = pltpu.roll(tile.astype(F32), SHELL, 1).astype(BF16)
        rows = pl.ds(pl.multiple_of(q * batch_rows + (parity * chips + source) * ROWS, ROWS), ROWS)
        for c in range(nu_tiles):
            one = places[parity, source, 0, 2 * c]
            two = places[parity, source, 0, 2 * c + 1]
            columns = slice(c * LANE, (c + 1) * LANE)
            half_y[rows, columns] = jnp.where(left, tiles[0, one], tiles[0, two])
            half_x[rows, columns] = jnp.where(left, tiles[1, one], tiles[1, two])

    way = 1 - 2 * odd
    whole = out_ring.shape[1]
    front = out_rest.shape[2]
    rest = (whole, padded - whole, 1)

    def pick_rows(t):
        for row, rows, sign in pieces + [rest]:
            lhs[row : row + rows, :] = vir_t[around(-sign * way * (t + 1)), row : row + rows, :]

    def column_cuts(step):
        return [(c, min(c + step, nu_w)) for c in range(0, nu_w, step)]

    pick_rows(0)

    @pl.loop(0, chunks)
    def _(q):
        spread_out(q, odd, chip)

        @pl.loop(1, chips)
        def _(d):
            data_copy(q, d).wait_recv()
            pass_copy(q, d).start()
            spread_out(q, odd, back(d))

        @pl.loop(0, chips)
        def _(d):
            pass_copy(q, d).wait_recv()
            spread_out(q, 1 - odd, back(d))

        rows = pl.ds(pl.multiple_of(q * batch_rows, ROWS), batch_rows)
        wide[:, :batch_rows] = lax.dot_general(
            lhs[...], half_y[rows, :], NT, preferred_element_type=F32
        ).astype(BF16)

        @pl.when(q == 0)
        def _():
            for low, high in column_cuts(256):
                own[:, low:high] = jnp.dot(wide[:, :batch_rows], half_x[rows, low:high], preferred_element_type=F32)

        @pl.when(q > 0)
        def _():
            for low, high in column_cuts(256):
                own[:, low:high] += jnp.dot(wide[:, :batch_rows], half_x[rows, low:high], preferred_element_type=F32)

    def ring_copy(t, k):
        if k == len(pieces):
            source, target = out_rest.at[t], in_rest.at[t]
            sign = 1
        else:
            row, rows, sign = pieces[k]
            source, target = out_ring.at[t, pl.ds(row, rows)], in_ring.at[t, pl.ds(row, rows)]
        return pltpu.make_async_remote_copy(
            source,
            target,
            ring_send.at[k, t],
            ring_recv.at[k, t],
            device_id={"occ": around(way * sign)},
            device_id_type=MESH,
        )

    def packed_rest():
        back_part = own[whole : whole + 8, front:]
        if back_part.shape[1] < front:
            back_part = jnp.concatenate([back_part, jnp.zeros((8, front - back_part.shape[1]), F32)], axis=1)
        return jnp.concatenate([own[whole : whole + 8, :front], back_part], axis=0)

    @pl.loop(0, n_occ)
    def _(t):
        @pl.when(t > 0)
        def _():
            pick_rows(t)
            for p in range(0, n_aux * slab, 256):
                end = min(p + 256, n_aux * slab)
                wide[:, p:end] = lax.dot_general(
                    lhs[...], half_y[p:end, :], NT, preferred_element_type=F32
                ).astype(BF16)
            for low, high in column_cuts(256):
                own[:, low:high] = jnp.dot(wide[...], half_x[:, low:high], preferred_element_type=F32)

        for k in range(len(pieces) + 1):
            if k < len(pieces):
                span = slice(pieces[k][0], pieces[k][0] + pieces[k][1])

            @pl.when(t == 0)
            def _():
                if k < len(pieces):
                    out_ring[t, span, :] = own[span, :].astype(BF16)
                else:
                    out_rest[t] = packed_rest().astype(BF16)

            @pl.when(t > 0)
            def _():
                ring_copy(t - 1, k).wait_recv()
                if k < len(pieces):
                    out_ring[t, span, :] = (own[span, :] + in_ring[t - 1, span, :].astype(F32)).astype(BF16)
                else:
                    out_rest[t] = (packed_rest() + in_rest[t - 1].astype(F32)).astype(BF16)

            @pl.when(t < n_occ - 1)
            def _():
                ring_copy(t, k).start()

    last = n_occ - 1
    total_u[:whole, :] = out_ring[last]
    packed = out_rest[last].astype(F32)
    unpacked = jnp.concatenate([packed[:8], packed[8:, : nu_w - front]], axis=1)
    total_u[whole:, :] = jnp.concatenate([unpacked, jnp.zeros((padded - whole - 8, nu_w), F32)], axis=0).astype(BF16)

    farthest = n_occ // 2
    far = farthest - 1
    far_block = around(farthest)
    nearer_half = g < farthest

    def tile_step(d):
        return way * (d if d % 2 == 1 else -d)

    def lead_copy(d):
        return pltpu.make_async_remote_copy(
            out_lead.at[d - 1],
            in_lead.at[d - 1],
            lead_send.at[d - 1],
            lead_recv.at[d - 1],
            device_id={"occ": around(tile_step(d))},
            device_id_type=MESH,
        )

    def tail_copy(d):
        return pltpu.make_async_remote_copy(
            out_tail.at[d - 1],
            in_tail.at[d - 1],
            tail_send.at[d - 1],
            tail_recv.at[d - 1],
            device_id={"occ": around(tile_step(d))},
            device_id_type=MESH,
        )

    def times(one, two):
        return lax.dot_general(one, two, NT, preferred_element_type=F32)

    @pl.when(nearer_half)
    def _():
        out_lead[far] = times(total_u[...], vir_t[far_block, :LANE, :]).astype(BF16)
        lead_copy(farthest).start()

    @pl.when(jnp.logical_not(nearer_half))
    def _():
        out_tail[far] = times(total_u[LANE:, :], vir_t[far_block]).astype(BF16)
        tail_copy(farthest).start()

    for d in range(far, 0, -1):
        to = around(tile_step(d))
        out_lead[d - 1] = times(total_u[...], vir_t[to, :LANE, :]).astype(BF16)
        lead_copy(d).start()
        out_tail[d - 1] = times(vir_t[to, LANE:, :], total_u[...]).astype(BF16)
        tail_copy(d).start()

    e_pair = eocc_ref[order_ref[a]] + eocc_ref[order_ref[lax.rem(a + n_aux - 1, n_aux)]]

    def e_row(h, low, high):
        return eblock[h][:, low:high]

    def e_column(h, low, high):
        return jnp.broadcast_to(eblock[h], (8, eblock.shape[2])).T[low:high, 0:1]

    e_rows = e_pair - e_column(g, 0, padded)
    total = jnp.zeros((8, LANE), F32)
    for c in range(0, nvir, 256):
        end = min(c + 256, nvir)
        pair = times(total_u[...], vir[c:end, :])
        ratio = pair / (e_rows - erow[:, c:end])
        amp_ref[0, :, c:end] = ratio[:width].astype(BF16)
        total = total + folded(ratio * (2.0 * pair))

    block = times(total_u[...], vir_t[g])
    same = times(vir_t[g], total_u[...])
    total = total - folded(block / (e_rows - e_row(g, 0, padded)) * same)

    def lead_ratio(h):
        under = (e_pair - e_column(h, 0, padded)) - e_row(g, 0, LANE)
        return times(vir_t[h], total_u[:LANE, :]) / under

    for d in range(1, farthest):
        source = around(-tile_step(d))
        ratio_lead[d - 1] = lead_ratio(source)
        ratio_tail[d - 1] = times(total_u[LANE:, :], vir_t[source]) / (e_rows[LANE:] - e_row(source, 0, padded))

    @pl.when(nearer_half)
    def _():
        under = (e_pair - e_column(far_block, LANE, padded)) - e_row(g, 0, padded)
        ratio_tail[far] = times(vir_t[far_block, LANE:, :], total_u[...]) / under

    @pl.when(jnp.logical_not(nearer_half))
    def _():
        ratio_lead[far] = lead_ratio(far_block)

    part[...] = total
    for d in range(1, farthest):
        lead_copy(d).wait_recv()
        tail_copy(d).wait_recv()
        met = folded(ratio_lead[d - 1] * in_lead[d - 1].astype(F32))
        part[...] -= 2.0 * (met + folded(ratio_tail[d - 1] * in_tail[d - 1].astype(F32)))

    @pl.when(nearer_half)
    def _():
        tail_copy(farthest).wait_recv()
        part[...] -= 2.0 * folded(ratio_tail[far] * in_tail[far].astype(F32))

    @pl.when(jnp.logical_not(nearer_half))
    def _():
        lead_copy(farthest).wait_recv()
        part[...] -= 2.0 * folded(ratio_lead[far] * in_lead[far].astype(F32))

    total = part[...]

    def part_copy(d):
        return pltpu.make_async_remote_copy(
            part, parts.at[d], part_send.at[d], part_recv.at[d], device_id={"occ": around(d)}, device_id_type=MESH
        )

    for d in sorted(range(1, n_occ), key=lambda d: -min(d, n_occ - d)):
        part_copy(d).start()
    for d in range(1, n_occ):
        part_copy(d).wait_recv()
        total = total + parts[d]
    energy_ref[0] = jnp.sum(total) / (nvir * nvir)

    for d in range(1, n_occ):
        part_copy(d).wait_send()
    for d in range(1, farthest):
        lead_copy(d).wait_send()
        tail_copy(d).wait_send()

    @pl.when(nearer_half)
    def _():
        lead_copy(farthest).wait_send()

    @pl.when(jnp.logical_not(nearer_half))
    def _():
        tail_copy(farthest).wait_send()

    @pl.loop(0, n_occ - 1)
    def _(t):
        for k in range(len(pieces) + 1):
            ring_copy(t, k).wait_send()

    meta_pass().wait_send()

    @pl.loop(1, chips)
    def _(d):
        meta_copy(d).wait_send()

    @pl.loop(0, chunks)
    def _(q):
        pass_copy(q, 0).wait_send()

        @pl.loop(1, chips)
        def _(d):
            data_copy(q, d).wait_send()
            pass_copy(q, d).wait_send()


def pair_results(
    n_aux, n_occ, integrals, mu_shells, nu_shells, block_count, occ_t, vir_t, occ_order, occ_energies, vir_energies
):
    slots, slab, _ = integrals.shape
    occ_count, nao = occ_t.shape
    nvir, nu_w = vir_t.shape
    width = nvir // n_occ
    padded = -(-width // ROWS) * ROWS
    chunks = slab // ROWS
    chips = n_aux // 2
    aux_rows = n_aux * slab
    farthest = n_occ // 2
    spread_rows = slots * SHELL * SHELL // LANE * ROWS
    mixed = slots * occ_count
    whole = width // ROWS * ROWS
    front = -(-nu_w // (2 * LANE)) * LANE
    cuts = [whole * k // (4 * ROWS) * ROWS for k in range(5)]
    spans = [(low, high - low, sign) for low, high, sign in zip(cuts[:-1], cuts[1:], (1, 1, -1, -1))]
    pieces = [spans[k] for k in (0, 2, 1, 3) if spans[k][1]]
    vmem = pl.BlockSpec(memory_space=pltpu.VMEM)
    smem = pl.BlockSpec(memory_space=pltpu.SMEM)
    anywhere = pl.BlockSpec(memory_space=pl.ANY)
    dma = pltpu.SemaphoreType.DMA
    macs = 2 * n_occ * padded * aux_rows * nu_w
    return pl.pallas_call(
        functools.partial(pair_kernel, n_aux, n_occ, pieces),
        in_specs=[anywhere, smem, smem, smem, anywhere, anywhere, smem, smem, vmem],
        out_specs=(vmem, smem),
        out_shape=(jax.ShapeDtypeStruct((1, width, nvir), BF16), jax.ShapeDtypeStruct((1,), F32)),
        scratch_shapes=[
            pltpu.VMEM((chunks, slots, ROWS, SHELL * SHELL), BF16),
            pltpu.VMEM((occ_count, nao), BF16),
            pltpu.VMEM((slots * SHELL, mixed), F32),
            pltpu.VMEM((mixed, slots * SHELL), BF16),
            pltpu.VMEM((spread_rows, LANE), F32),
            pltpu.VMEM((HALF * mixed, LANE), F32),
            pltpu.VMEM((chunks, occ_count + 1, ROWS, slots * SHELL), BF16),
            pltpu.VMEM((2, chips, chunks, 3, ROWS, slots * SHELL), BF16),
            pltpu.VMEM((8, LANE), I32),
            pltpu.VMEM((2, chips, 8, LANE), I32),
            pltpu.SMEM((2, chips, 8, LANE), I32),
            pltpu.VMEM((2, slots + 1, ROWS, LANE), BF16),
            pltpu.VMEM((aux_rows, nu_w), BF16),
            pltpu.VMEM((aux_rows, nu_w), BF16),
            pltpu.VMEM((nvir, nu_w), BF16),
            pltpu.VMEM((n_occ, padded, nu_w), BF16),
            pltpu.VMEM((1, nvir), F32),
            pltpu.VMEM((n_occ, 1, -(-padded // LANE) * LANE), F32),
            pltpu.VMEM((padded, nu_w), BF16),
            pltpu.VMEM((padded, aux_rows), BF16),
            pltpu.VMEM((padded, nu_w), F32),
            pltpu.VMEM((n_occ, whole, nu_w), BF16),
            pltpu.VMEM((n_occ - 1, whole, nu_w), BF16),
            pltpu.VMEM((n_occ, ROWS, front), BF16),
            pltpu.VMEM((n_occ - 1, ROWS, front), BF16),
            pltpu.VMEM((padded, nu_w), BF16),
            pltpu.VMEM((farthest, padded, LANE), BF16),
            pltpu.VMEM((farthest, padded, LANE), BF16),
            pltpu.VMEM((farthest, padded - LANE, padded), BF16),
            pltpu.VMEM((farthest, padded - LANE, padded), BF16),
            pltpu.VMEM((farthest, padded, LANE), F32),
            pltpu.VMEM((farthest, padded - LANE, padded), F32),
            pltpu.VMEM((8, LANE), F32),
            pltpu.VMEM((n_occ, 8, LANE), F32),
            dma((chunks + 3,)),
            dma((chunks,)),
            dma((chips,)),
            dma((chips,)),
            dma((chunks, chips)),
            dma((chunks, chips)),
            dma((chunks, chips)),
            dma((chunks, chips)),
            dma((len(pieces) + 1, n_occ - 1)),
            dma((len(pieces) + 1, n_occ - 1)),
            dma((farthest,)),
            dma((farthest,)),
            dma((farthest,)),
            dma((farthest,)),
            dma((n_occ,)),
            dma((n_occ,)),
        ],
        compiler_params=pltpu.CompilerParams(
            collective_id=0, has_side_effects=True, vmem_limit_bytes=60 * 2**20
        ),
        cost_estimate=pl.CostEstimate(flops=2 * macs, bytes_accessed=2 * nu_w * nvir, transcendentals=0),
    )(integrals, mu_shells, nu_shells, block_count, occ_t, vir_t, occ_order, occ_energies, vir_energies)


def local(
    n_aux,
    n_occ,
    integrals,
    mu_shells,
    nu_shells,
    block_count,
    occ_coeffs,
    vir_coeffs,
    occ_order,
    occ_energies,
    vir_energies,
):
    return pair_results(
        n_aux,
        n_occ,
        integrals[0],
        mu_shells,
        nu_shells,
        block_count,
        occ_coeffs.T,
        vir_coeffs.T,
        occ_order,
        occ_energies,
        vir_energies,
    )


def solution(mesh):
    placed = (
        P(("aux", "occ"), None, None, None),
        P(("aux", "occ"), None),
        P(("aux", "occ"), None),
        P(("aux", "occ")),
        P(),
        P(),
        P(),
        P(),
        P(),
    )
    return jax.shard_map(
        functools.partial(local, mesh.shape["aux"], mesh.shape["occ"]),
        mesh=mesh,
        in_specs=placed,
        out_specs=(P("aux", "occ", None), P("aux")),
        check_vma=False,
    )
```

```python
import functools

import jax
import jax.numpy as jnp
from jax import lax
from jax.experimental import pallas as pl
from jax.experimental.pallas import tpu as pltpu
from jax.sharding import PartitionSpec as P

SHELL = 64
LANE = 128
ROWS = 16
HALF = ROWS // 2
MESH = pl.DeviceIdType.MESH
F32 = jnp.float32
BF16 = jnp.bfloat16
I32 = jnp.int32
NT = (((1,), (1,)), ((), ()))


def left_half(shape):
    return lax.broadcasted_iota(I32, shape, len(shape) - 1) < SHELL


def iota(shape, dim):
    return lax.broadcasted_iota(I32, shape, dim)


def halves_apart(one, two, left):
    turned = pltpu.roll(jnp.where(left, two, one), SHELL, 1)
    return [jnp.where(left, one, turned), jnp.where(left, turned, two)]


def first_of_kind(slots, nu_ref, count):
    live = [k < count for k in range(slots)]
    first = []
    for k in range(slots):
        new = live[k]
        for j in range(k):
            new = new & (nu_ref[0, j] != nu_ref[0, k])
        first.append(new)
    return live, first


def build_mixer(slots, occ_count, mu_ref, nu_ref, order_ref, live, first, occ, tall, mixer):
    lane_tiles = SHELL * SHELL // LANE
    depth = slots * lane_tiles
    wide = slots * occ_count
    lane = iota((1, wide), 1)
    batch = lane % occ_count
    target = lane // occ_count
    order = jnp.zeros((1, wide), I32)
    for i in range(occ_count):
        order = jnp.where(batch == i, order_ref[i], order)
    shell = jnp.full((1, wide), -1, I32)
    for k in range(slots):
        shell = jnp.where(target == k, jnp.where(first[k], nu_ref[0, k], -1), shell)
    picked = iota((occ_count, wide), 0) == order
    row = iota((SHELL, LANE), 0)
    col = iota((SHELL, LANE), 1)
    wanted = 2 * (row % lane_tiles) + row // lane_tiles
    for k in range(slots):
        mu = mu_ref[0, k]
        rows = occ[:, :LANE]
        for t in range(1, occ.shape[1] // LANE):
            rows = jnp.where(mu // 2 == t, occ[:, t * LANE : (t + 1) * LANE], rows)
        split = (col == wanted + mu % 2 * SHELL).astype(F32).astype(BF16)
        parted = lax.dot_general(split, rows, NT, preferred_element_type=F32).astype(BF16)
        here = jnp.where(live[k], nu_ref[0, k], -2)
        picker = (picked & (shell == here)).astype(F32).astype(BF16)
        both = jnp.dot(parted, picker, preferred_element_type=F32)
        tall[k * lane_tiles : (k + 1) * lane_tiles, :] = both[:lane_tiles]
        tall[depth + k * lane_tiles : depth + (k + 1) * lane_tiles, :] = both[lane_tiles:]
    mixer[...] = tall[...].T.astype(BF16)


def place_table(slots, nu_ref, first):
    shell = iota((8, LANE), 1)
    place = jnp.full((8, LANE), slots, I32)
    for k in range(slots):
        here = jnp.where(first[k], nu_ref[0, k], -1)
        turned = jnp.where(shell % 2 == k % 2, k // 2, slots // 2 + k // 2)
        place = jnp.where(shell == here, turned, place)
    return place


def half_transform(slots, occ_count, q, blocks, mixer, spread, prods, ext):
    lane_tiles = SHELL * SHELL // LANE
    depth = slots * lane_tiles
    wide = slots * occ_count

    @pl.loop(0, slots)
    def _(k):
        for t in range(lane_tiles):
            at = pl.multiple_of((k * lane_tiles + t) * ROWS, ROWS)
            spread[pl.ds(at, ROWS), :] = blocks[q, k, :, t * LANE : (t + 1) * LANE].astype(F32)

    left = left_half((depth, LANE))
    for r in range(0, HALF, 2):
        columns = []
        for e in range(2):
            one = spread[pl.ds(r + e, depth, stride=ROWS), :]
            two = spread[pl.ds(r + e + HALF, depth, stride=ROWS), :]
            columns.append(jnp.concatenate(halves_apart(one, two, left), axis=0).astype(BF16))
        both = jnp.dot(mixer[...], jnp.concatenate(columns, axis=1), preferred_element_type=F32)
        for e in range(2):
            prods[(r + e) * wide : (r + e + 1) * wide, :] = both[:, e * LANE : (e + 1) * LANE]

    left = left_half((HALF, LANE))
    for i in range(occ_count + 1):
        batch = (i - 1) % occ_count
        for s in range(slots // 2):
            one = prods[pl.ds(2 * s * occ_count + batch, HALF, stride=wide), :]
            two = prods[pl.ds((2 * s + 1) * occ_count + batch, HALF, stride=wide), :]
            pair = jnp.concatenate(halves_apart(one, two, left), axis=0)
            ext[q, i, :, s * LANE : (s + 1) * LANE] = pair.astype(BF16)


def folded(values):
    rows, cols = values.shape
    if cols % LANE:
        values = jnp.concatenate([values, jnp.zeros((rows, LANE - cols % LANE), F32)], axis=1)
    result = values[:, :LANE]
    for c in range(LANE, values.shape[1], LANE):
        result = result + values[:, c : c + LANE]
    return jnp.sum(result.reshape(rows // 8, 8, LANE), axis=0)


def pair_kernel(
    n_aux,
    n_occ,
    pieces,
    integrals_ref,
    mu_ref,
    nu_ref,
    count_ref,
    occ_ref,
    vir_ref,
    order_ref,
    eocc_ref,
    evir_ref,
    amp_ref,
    energy_ref,
    amp,
    blocks,
    occ,
    tall,
    mixer,
    spread,
    prods,
    ext,
    got,
    meta,
    metas,
    places,
    tiles,
    half_y,
    half_x,
    vir,
    vir_t,
    erow,
    eblock,
    lhs,
    wide,
    own,
    out_ring,
    in_ring,
    out_rest,
    in_rest,
    total_u,
    out_lead,
    in_lead,
    out_tail,
    in_tail,
    ratio_lead,
    ratio_tail,
    part,
    parts,
    local_sem,
    keep_sem,
    meta_send,
    meta_recv,
    data_send,
    data_recv,
    single_send,
    single_recv,
    pass_send,
    pass_recv,
    ring_send,
    ring_recv,
    lead_send,
    lead_recv,
    tail_send,
    tail_recv,
    part_send,
    part_recv,
):
    a = lax.axis_index("aux")
    g = lax.axis_index("occ")
    odd = lax.rem(a, 2)
    chip = a // 2
    mate = a + 1 - 2 * odd
    chips = n_aux // 2
    slots = blocks.shape[1]
    chunks = blocks.shape[0]
    occ_count = occ.shape[0]
    nvir, nu_w = vir.shape
    width = nvir // n_occ
    padded = vir_t.shape[1]
    slab = chunks * ROWS
    packs = slots // 2
    nu_tiles = nu_w // LANE

    def near(step):
        if chips != 16:
            return lax.rem(chip + step + chips, chips)
        return lax.rem(chip // 4 + step // 4, 4) * 4 + lax.rem(chip + step, 4)

    def back(step):
        if chips != 16:
            return lax.rem(chip - step + chips, chips)
        return lax.rem(chip // 4 - step // 4 + 4, 4) * 4 + lax.rem(chip % 4 - step % 4 + 4, 4)

    def around(step):
        return lax.rem(g + step + 2 * n_occ, n_occ)

    loads = [pltpu.make_async_copy(occ_ref, occ, local_sem.at[0])]
    for q in range(chunks):
        loads.append(
            pltpu.make_async_copy(integrals_ref.at[:, pl.ds(q * ROWS, ROWS)], blocks.at[q], local_sem.at[q + 1])
        )
    load_vir = pltpu.make_async_copy(vir_ref, vir, local_sem.at[chunks + 1])
    for load in loads:
        load.start()
    load_vir.start()

    barrier = pltpu.get_barrier_semaphore()

    @pl.loop(1, chips)
    def _(d):
        pl.semaphore_signal(barrier, inc=1, device_id={"aux": 2 * near(d) + odd}, device_id_type=MESH)

    pl.semaphore_signal(barrier, inc=1, device_id={"aux": mate}, device_id_type=MESH)

    @pl.loop(1, n_occ)
    def _(d):
        pl.semaphore_signal(barrier, inc=1, device_id={"occ": around(d)}, device_id_type=MESH)

    live, first = first_of_kind(slots, nu_ref, count_ref[0])
    meta[...] = place_table(slots, nu_ref, first)
    metas[odd, chip] = meta[...]
    loads[0].wait()
    build_mixer(slots, occ_count, mu_ref, nu_ref, order_ref, live, first, occ, tall, mixer)

    def meta_copy(d):
        return pltpu.make_async_remote_copy(
            meta,
            metas.at[odd, chip],
            meta_send.at[d],
            meta_recv.at[d],
            device_id={"aux": 2 * near(d) + odd},
            device_id_type=MESH,
        )

    def meta_pass():
        return pltpu.make_async_remote_copy(
            metas.at[odd], metas.at[odd], meta_send.at[0], meta_recv.at[0], device_id={"aux": mate}, device_id_type=MESH
        )

    def data_copy(q, d):
        to = near(d)
        return pltpu.make_async_remote_copy(
            ext.at[q, pl.ds(2 * to, 2)],
            got.at[odd, chip, q, pl.ds(0, 2)],
            data_send.at[q, d],
            data_recv.at[q, d],
            device_id={"aux": 2 * to + odd},
            device_id_type=MESH,
        )

    def single_copy(parity, d):
        to = near(d)
        return pltpu.make_async_remote_copy(
            ext.at[:, 2 * to + 2],
            got.at[odd, chip, :, 2],
            single_send.at[d],
            single_recv.at[parity, d],
            device_id={"aux": 2 * to + 1},
            device_id_type=MESH,
        )

    def keep_copy(q):
        return pltpu.make_async_copy(ext.at[q, pl.ds(2 * chip, 3)], got.at[odd, chip, q], keep_sem.at[q])

    def pass_copy(d):
        view = got.at[odd, back(d), :, pl.ds(0, 2)]
        return pltpu.make_async_remote_copy(
            view, view, pass_send.at[d], pass_recv.at[d], device_id={"aux": mate}, device_id_type=MESH
        )

    @pl.loop(0, chunks)
    def _(q):
        pltpu.make_async_copy(
            integrals_ref.at[:, pl.ds(pl.multiple_of(q * ROWS, ROWS), ROWS)], blocks.at[q], local_sem.at[q + 1]
        ).wait()
        half_transform(slots, occ_count, q, blocks, mixer, spread, prods, ext)
        keep_copy(q).start()

        @pl.when(q == 0)
        def _():
            pl.semaphore_wait(barrier, chips + n_occ - 1)

            @pl.loop(1, chips)
            def _(d):
                meta_copy(d).start()

        @pl.loop(1, chips)
        def _(d):
            data_copy(q, d).start()

    @pl.loop(1, chips)
    def _(d):
        meta_copy(d).wait_recv()

    meta_pass().start()
    tiles[:, 2 * packs] = jnp.zeros((2, slab, LANE), BF16)
    load_vir.wait()

    def block_vir(c):
        low = c * width // ROWS * ROWS
        high = -(-(c + 1) * width // ROWS) * ROWS
        off = c * width - low
        for w in range(0, nu_w, LANE):
            rows = vir[low:high, w : w + LANE].astype(F32)[off : off + width]
            if padded > width:
                rows = jnp.concatenate([rows, jnp.zeros((padded - width, LANE), F32)], axis=0)
            vir_t[c, :, w : w + LANE] = rows.astype(BF16)

    for c in range(n_occ // 2):
        block_vir(c)
    meta_pass().wait_recv()
    placing = pltpu.make_async_copy(metas, places, local_sem.at[chunks + 2])
    placing.start()
    for c in range(n_occ // 2, n_occ):
        block_vir(c)
    erow[...] = evir_ref[...].reshape(1, nvir)
    for c in range(n_occ):
        eblock[c] = jnp.concatenate(
            [erow[:, c * width : (c + 1) * width], jnp.ones((1, eblock.shape[2] - width), F32)], axis=1
        )

    for q in range(chunks):
        keep_copy(q).wait()
    pass_copy(0).start()
    placing.wait()

    left = left_half((slab, LANE))

    halves = (half_y, half_x)

    def spread_sides(d, parity, sides):
        source = back(d)
        for side, slot in sides:
            for s in range(packs):
                tile = got[parity, source, :, slot, :, s * LANE : (s + 1) * LANE].reshape(slab, LANE)
                tiles[side, s] = tile
                tiles[side, packs + s] = pltpu.roll(tile.astype(F32), SHELL, 1).astype(BF16)
        rows = pl.ds(pl.multiple_of((2 * d + parity) * slab, ROWS), slab)
        for c in range(nu_tiles):
            one = places[parity, source, 0, 2 * c]
            two = places[parity, source, 0, 2 * c + 1]
            for side, _ in sides:
                halves[side][rows, c * LANE : (c + 1) * LANE] = jnp.where(left, tiles[side, one], tiles[side, two])

    def spread_out(d, parity):
        @pl.when(odd == 0)
        def _():
            spread_sides(d, parity, ((0, 0), (1, 1)))

        @pl.when(odd == 1)
        def _():
            spread_sides(d, parity, ((0, 1),))

    way = 1 - 2 * odd
    whole = out_ring.shape[1]
    front = out_rest.shape[2]
    rest = (whole, padded - whole, 1)

    def times(one, two):
        return lax.dot_general(one, two, NT, preferred_element_type=F32)

    def pick_rows(t):
        for row, rows, sign in pieces + [rest]:
            lhs[row : row + rows, :] = vir_t[around(-sign * way * (t + 1)), row : row + rows, :]

    def column_cuts(step):
        return [(c, min(c + step, nu_w)) for c in range(0, nu_w, step)]

    pick_rows(0)

    group = max(1, chips // 4)
    group_rows = 2 * group * slab

    def rows_of(k):
        return pl.ds(pl.multiple_of(k * group_rows, group_rows), group_rows)

    def add_products(k):
        rows = rows_of(k)

        @pl.when(k == 0)
        def _():
            for low, high in column_cuts(256):
                own[:, low:high] = jnp.dot(wide[:, rows], half_x[rows, low:high], preferred_element_type=F32)

        @pl.when(k > 0)
        def _():
            for low, high in column_cuts(256):
                own[:, low:high] += jnp.dot(wide[:, rows], half_x[rows, low:high], preferred_element_type=F32)

    @pl.loop(0, chips // group)
    def _(k):
        @pl.loop(0, group)
        def _(step):
            d = k * group + step

            @pl.when(d == min(0, chips - 1))
            def _():
                @pl.when(odd == 0)
                def _():
                    single_copy(0, 0).start()

                @pl.loop(1, chips)
                def _(e):
                    single_copy(odd, e).start()

            @pl.when(d > 0)
            def _():
                @pl.loop(0, chunks)
                def _(q):
                    data_copy(q, d).wait_recv()

                pass_copy(d).start()

            spread_out(d, odd)

            @pl.when(step > 0)
            def _():
                pass_copy(d - 1).wait_recv()
                spread_out(d - 1, 1 - odd)

        pass_copy(k * group + group - 1).wait_recv()
        spread_out(k * group + group - 1, 1 - odd)
        rows = rows_of(k)
        wide[:, rows] = times(lhs[...], half_y[rows, :]).astype(BF16)

        @pl.when(odd == 0)
        def _():
            add_products(k)

    @pl.when(odd == 1)
    def _():
        @pl.loop(0, chips // group)
        def _(k):
            @pl.loop(0, group)
            def _(step):
                d = k * group + step
                single_copy(0, d).wait_recv()
                spread_sides(d, 0, ((1, 2),))

                @pl.when(d > 0)
                def _():
                    single_copy(1, d).wait_recv()

                spread_sides(d, 1, ((1, 2),))

            add_products(k)

    def ring_copy(t, k):
        if k == len(pieces):
            source, target = out_rest.at[t], in_rest.at[t]
            sign = 1
        else:
            row, rows, sign = pieces[k]
            source, target = out_ring.at[t, pl.ds(row, rows)], in_ring.at[t, pl.ds(row, rows)]
        return pltpu.make_async_remote_copy(
            source,
            target,
            ring_send.at[k, t],
            ring_recv.at[k, t],
            device_id={"occ": around(way * sign)},
            device_id_type=MESH,
        )

    def packed_rest():
        back_part = own[whole : whole + 8, front:]
        if back_part.shape[1] < front:
            back_part = jnp.concatenate([back_part, jnp.zeros((8, front - back_part.shape[1]), F32)], axis=1)
        return jnp.concatenate([own[whole : whole + 8, :front], back_part], axis=0)

    @pl.loop(0, n_occ)
    def _(t):
        @pl.when(t > 0)
        def _():
            pick_rows(t)
            for p in range(0, n_aux * slab, 256):
                end = min(p + 256, n_aux * slab)
                wide[:, p:end] = lax.dot_general(
                    lhs[...], half_y[p:end, :], NT, preferred_element_type=F32
                ).astype(BF16)
            for low, high in column_cuts(256):
                own[:, low:high] = jnp.dot(wide[...], half_x[:, low:high], preferred_element_type=F32)

        for k in range(len(pieces) + 1):
            if k < len(pieces):
                span = slice(pieces[k][0], pieces[k][0] + pieces[k][1])

            @pl.when(t == 0)
            def _():
                if k < len(pieces):
                    out_ring[t, span, :] = own[span, :].astype(BF16)
                else:
                    out_rest[t] = packed_rest().astype(BF16)

            @pl.when(t > 0)
            def _():
                ring_copy(t - 1, k).wait_recv()
                if k < len(pieces):
                    out_ring[t, span, :] = (own[span, :] + in_ring[t - 1, span, :].astype(F32)).astype(BF16)
                else:
                    out_rest[t] = (packed_rest() + in_rest[t - 1].astype(F32)).astype(BF16)

            @pl.when(t < n_occ - 1)
            def _():
                ring_copy(t, k).start()

    last = n_occ - 1
    total_u[:whole, :] = out_ring[last]
    packed = out_rest[last].astype(F32)
    unpacked = jnp.concatenate([packed[:8], packed[8:, : nu_w - front]], axis=1)
    total_u[whole:, :] = jnp.concatenate([unpacked, jnp.zeros((padded - whole - 8, nu_w), F32)], axis=0).astype(BF16)

    farthest = n_occ // 2
    far = farthest - 1
    far_block = around(farthest)
    nearer_half = g < farthest

    def tile_step(d):
        return way * (d if d % 2 == 1 else -d)

    def lead_copy(d):
        return pltpu.make_async_remote_copy(
            out_lead.at[d - 1],
            in_lead.at[d - 1],
            lead_send.at[d - 1],
            lead_recv.at[d - 1],
            device_id={"occ": around(tile_step(d))},
            device_id_type=MESH,
        )

    def tail_copy(d):
        return pltpu.make_async_remote_copy(
            out_tail.at[d - 1],
            in_tail.at[d - 1],
            tail_send.at[d - 1],
            tail_recv.at[d - 1],
            device_id={"occ": around(tile_step(d))},
            device_id_type=MESH,
        )

    @pl.when(nearer_half)
    def _():
        out_lead[far] = times(total_u[...], vir_t[far_block, :LANE, :]).astype(BF16)
        lead_copy(farthest).start()

    @pl.when(jnp.logical_not(nearer_half))
    def _():
        out_tail[far] = times(total_u[LANE:, :], vir_t[far_block]).astype(BF16)
        tail_copy(farthest).start()

    for d in range(far, 0, -1):
        to = around(tile_step(d))
        out_lead[d - 1] = times(total_u[...], vir_t[to, :LANE, :]).astype(BF16)
        lead_copy(d).start()
        out_tail[d - 1] = times(vir_t[to, LANE:, :], total_u[...]).astype(BF16)
        tail_copy(d).start()

    e_pair = eocc_ref[order_ref[a]] + eocc_ref[order_ref[lax.rem(a + n_aux - 1, n_aux)]]

    def e_row(h, low, high):
        return eblock[h][:, low:high]

    def e_column(h, low, high):
        return jnp.broadcast_to(eblock[h], (8, eblock.shape[2])).T[low:high, 0:1]

    e_rows = e_pair - e_column(g, 0, padded)
    total = jnp.zeros((8, LANE), F32)
    for c in range(0, nvir, 256):
        end = min(c + 256, nvir)
        pair = times(total_u[...], vir[c:end, :])
        ratio = pair / (e_rows - erow[:, c:end])
        amp[0, :, c:end] = ratio[:width].astype(BF16)
        total = total + folded(ratio * (2.0 * pair))
    leaving = pltpu.make_async_copy(amp, amp_ref, local_sem.at[0])
    leaving.start()

    block = times(total_u[...], vir_t[g])
    same = times(vir_t[g], total_u[...])
    total = total - folded(block / (e_rows - e_row(g, 0, padded)) * same)

    def lead_ratio(h):
        under = (e_pair - e_column(h, 0, padded)) - e_row(g, 0, LANE)
        return times(vir_t[h], total_u[:LANE, :]) / under

    for d in range(1, farthest):
        source = around(-tile_step(d))
        ratio_lead[d - 1] = lead_ratio(source)
        ratio_tail[d - 1] = times(total_u[LANE:, :], vir_t[source]) / (e_rows[LANE:] - e_row(source, 0, padded))

    @pl.when(nearer_half)
    def _():
        under = (e_pair - e_column(far_block, LANE, padded)) - e_row(g, 0, padded)
        ratio_tail[far] = times(vir_t[far_block, LANE:, :], total_u[...]) / under

    @pl.when(jnp.logical_not(nearer_half))
    def _():
        ratio_lead[far] = lead_ratio(far_block)

    part[...] = total
    for d in range(1, farthest):
        lead_copy(d).wait_recv()
        tail_copy(d).wait_recv()
        met = folded(ratio_lead[d - 1] * in_lead[d - 1].astype(F32))
        part[...] -= 2.0 * (met + folded(ratio_tail[d - 1] * in_tail[d - 1].astype(F32)))

    @pl.when(nearer_half)
    def _():
        tail_copy(farthest).wait_recv()
        part[...] -= 2.0 * folded(ratio_tail[far] * in_tail[far].astype(F32))

    @pl.when(jnp.logical_not(nearer_half))
    def _():
        lead_copy(farthest).wait_recv()
        part[...] -= 2.0 * folded(ratio_lead[far] * in_lead[far].astype(F32))

    total = part[...]

    def part_copy(d):
        return pltpu.make_async_remote_copy(
            part, parts.at[d], part_send.at[d], part_recv.at[d], device_id={"occ": around(d)}, device_id_type=MESH
        )

    for d in sorted(range(1, n_occ), key=lambda d: -min(d, n_occ - d)):
        part_copy(d).start()
    for d in range(1, n_occ):
        part_copy(d).wait_recv()
        total = total + parts[d]
    energy_ref[0] = jnp.sum(total) / (nvir * nvir)

    leaving.wait()
    for d in range(1, n_occ):
        part_copy(d).wait_send()
    for d in range(1, farthest):
        lead_copy(d).wait_send()
        tail_copy(d).wait_send()

    @pl.when(nearer_half)
    def _():
        lead_copy(farthest).wait_send()

    @pl.when(jnp.logical_not(nearer_half))
    def _():
        tail_copy(farthest).wait_send()

    @pl.loop(0, n_occ - 1)
    def _(t):
        for k in range(len(pieces) + 1):
            ring_copy(t, k).wait_send()

    meta_pass().wait_send()

    @pl.loop(1, chips)
    def _(d):
        meta_copy(d).wait_send()

    @pl.loop(0, chunks)
    def _(q):
        @pl.loop(1, chips)
        def _(d):
            data_copy(q, d).wait_send()

    @pl.loop(0, chips)
    def _(d):
        pass_copy(d).wait_send()

    @pl.when(odd == 0)
    def _():
        single_copy(0, 0).wait_send()

    @pl.loop(1, chips)
    def _(d):
        single_copy(odd, d).wait_send()


def pair_results(
    n_aux, n_occ, integrals, mu_shells, nu_shells, block_count, occ_t, vir_t, occ_order, occ_energies, vir_energies
):
    slots, slab, _ = integrals.shape
    occ_count, nao = occ_t.shape
    nvir, nu_w = vir_t.shape
    width = nvir // n_occ
    padded = -(-width // ROWS) * ROWS
    chunks = slab // ROWS
    chips = n_aux // 2
    aux_rows = n_aux * slab
    farthest = n_occ // 2
    spread_rows = slots * SHELL * SHELL // LANE * ROWS
    mixed = slots * occ_count
    whole = width // ROWS * ROWS
    front = -(-nu_w // (2 * LANE)) * LANE
    middle = whole // (2 * ROWS) * ROWS
    step = 32
    ahead = [(row, min(step, middle - row), 1) for row in range(0, middle, step)]
    behind = [(row, min(step, whole - row), -1) for row in range(middle, whole, step)]
    pieces = [piece for both in zip(ahead, behind) for piece in both]
    vmem = pl.BlockSpec(memory_space=pltpu.VMEM)
    smem = pl.BlockSpec(memory_space=pltpu.SMEM)
    anywhere = pl.BlockSpec(memory_space=pl.ANY)
    dma = pltpu.SemaphoreType.DMA
    macs = 2 * n_occ * padded * aux_rows * nu_w
    return pl.pallas_call(
        functools.partial(pair_kernel, n_aux, n_occ, pieces),
        in_specs=[anywhere, smem, smem, smem, anywhere, anywhere, smem, smem, vmem],
        out_specs=(anywhere, smem),
        out_shape=(jax.ShapeDtypeStruct((1, width, nvir), BF16), jax.ShapeDtypeStruct((1,), F32)),
        scratch_shapes=[
            pltpu.VMEM((1, width, nvir), BF16),
            pltpu.VMEM((chunks, slots, ROWS, SHELL * SHELL), BF16),
            pltpu.VMEM((occ_count, nao), BF16),
            pltpu.VMEM((slots * SHELL, mixed), F32),
            pltpu.VMEM((mixed, slots * SHELL), BF16),
            pltpu.VMEM((spread_rows, LANE), F32),
            pltpu.VMEM((HALF * mixed, LANE), F32),
            pltpu.VMEM((chunks, occ_count + 1, ROWS, slots * SHELL), BF16),
            pltpu.VMEM((2, chips, chunks, 3, ROWS, slots * SHELL), BF16),
            pltpu.VMEM((8, LANE), I32),
            pltpu.VMEM((2, chips, 8, LANE), I32),
            pltpu.SMEM((2, chips, 8, LANE), I32),
            pltpu.VMEM((2, slots + 1, slab, LANE), BF16),
            pltpu.VMEM((aux_rows, nu_w), BF16),
            pltpu.VMEM((aux_rows, nu_w), BF16),
            pltpu.VMEM((nvir, nu_w), BF16),
            pltpu.VMEM((n_occ, padded, nu_w), BF16),
            pltpu.VMEM((1, nvir), F32),
            pltpu.VMEM((n_occ, 1, -(-padded // LANE) * LANE), F32),
            pltpu.VMEM((padded, nu_w), BF16),
            pltpu.VMEM((padded, aux_rows), BF16),
            pltpu.VMEM((padded, nu_w), F32),
            pltpu.VMEM((n_occ, whole, nu_w), BF16),
            pltpu.VMEM((n_occ - 1, whole, nu_w), BF16),
            pltpu.VMEM((n_occ, ROWS, front), BF16),
            pltpu.VMEM((n_occ - 1, ROWS, front), BF16),
            pltpu.VMEM((padded, nu_w), BF16),
            pltpu.VMEM((farthest, padded, LANE), BF16),
            pltpu.VMEM((farthest, padded, LANE), BF16),
            pltpu.VMEM((farthest, padded - LANE, padded), BF16),
            pltpu.VMEM((farthest, padded - LANE, padded), BF16),
            pltpu.VMEM((farthest, padded, LANE), F32),
            pltpu.VMEM((farthest, padded - LANE, padded), F32),
            pltpu.VMEM((8, LANE), F32),
            pltpu.VMEM((n_occ, 8, LANE), F32),
            dma((chunks + 3,)),
            dma((chunks,)),
            dma((chips,)),
            dma((chips,)),
            dma((chunks, chips)),
            dma((chunks, chips)),
            dma((chips,)),
            dma((2, chips)),
            dma((chips,)),
            dma((chips,)),
            dma((len(pieces) + 1, n_occ - 1)),
            dma((len(pieces) + 1, n_occ - 1)),
            dma((farthest,)),
            dma((farthest,)),
            dma((farthest,)),
            dma((farthest,)),
            dma((n_occ,)),
            dma((n_occ,)),
        ],
        compiler_params=pltpu.CompilerParams(
            collective_id=0, has_side_effects=True, vmem_limit_bytes=60 * 2**20
        ),
        cost_estimate=pl.CostEstimate(flops=2 * macs, bytes_accessed=2 * nu_w * nvir, transcendentals=0),
    )(integrals, mu_shells, nu_shells, block_count, occ_t, vir_t, occ_order, occ_energies, vir_energies)


def local(
    n_aux,
    n_occ,
    integrals,
    mu_shells,
    nu_shells,
    block_count,
    occ_coeffs,
    vir_coeffs,
    occ_order,
    occ_energies,
    vir_energies,
):
    return pair_results(
        n_aux,
        n_occ,
        integrals[0],
        mu_shells,
        nu_shells,
        block_count,
        occ_coeffs.T,
        vir_coeffs.T,
        occ_order,
        occ_energies,
        vir_energies,
    )


def solution(mesh):
    placed = (
        P(("aux", "occ"), None, None, None),
        P(("aux", "occ"), None),
        P(("aux", "occ"), None),
        P(("aux", "occ")),
        P(),
        P(),
        P(),
        P(),
        P(),
    )
    return jax.shard_map(
        functools.partial(local, mesh.shape["aux"], mesh.shape["occ"]),
        mesh=mesh,
        in_specs=placed,
        out_specs=(P("aux", "occ", None), P("aux")),
        check_vma=False,
    )
```

```python
import functools

import jax
import jax.numpy as jnp
from jax import lax
from jax.experimental import pallas as pl
from jax.experimental.pallas import tpu as pltpu
from jax.sharding import PartitionSpec as P

SHELL = 64
LANE = 128
ROWS = 16
HALF = ROWS // 2
MESH = pl.DeviceIdType.MESH
F32 = jnp.float32
BF16 = jnp.bfloat16
I32 = jnp.int32
NT = (((1,), (1,)), ((), ()))


def left_half(shape):
    return lax.broadcasted_iota(I32, shape, len(shape) - 1) < SHELL


def iota(shape, dim):
    return lax.broadcasted_iota(I32, shape, dim)


def halves_apart(one, two, left):
    turned = pltpu.roll(jnp.where(left, two, one), SHELL, 1)
    return [jnp.where(left, one, turned), jnp.where(left, turned, two)]


def first_of_kind(slots, nu_ref, count):
    live = [k < count for k in range(slots)]
    first = []
    for k in range(slots):
        new = live[k]
        for j in range(k):
            new = new & (nu_ref[0, j] != nu_ref[0, k])
        first.append(new)
    return live, first


def build_mixer(slots, occ_count, mu_ref, nu_ref, order_ref, live, first, occ, tall, mixer):
    lane_tiles = SHELL * SHELL // LANE
    depth = slots * lane_tiles
    wide = slots * occ_count
    lane = iota((1, wide), 1)
    batch = lane % occ_count
    target = lane // occ_count
    order = jnp.zeros((1, wide), I32)
    for i in range(occ_count):
        order = jnp.where(batch == i, order_ref[i], order)
    shell = jnp.full((1, wide), -1, I32)
    for k in range(slots):
        shell = jnp.where(target == k, jnp.where(first[k], nu_ref[0, k], -1), shell)
    picked = iota((occ_count, wide), 0) == order
    row = iota((SHELL, LANE), 0)
    col = iota((SHELL, LANE), 1)
    wanted = 2 * (row % lane_tiles) + row // lane_tiles
    for k in range(slots):
        mu = mu_ref[0, k]
        rows = occ[:, :LANE]
        for t in range(1, occ.shape[1] // LANE):
            rows = jnp.where(mu // 2 == t, occ[:, t * LANE : (t + 1) * LANE], rows)
        split = (col == wanted + mu % 2 * SHELL).astype(F32).astype(BF16)
        parted = lax.dot_general(split, rows, NT, preferred_element_type=F32).astype(BF16)
        here = jnp.where(live[k], nu_ref[0, k], -2)
        picker = (picked & (shell == here)).astype(F32).astype(BF16)
        both = jnp.dot(parted, picker, preferred_element_type=F32)
        tall[k * lane_tiles : (k + 1) * lane_tiles, :] = both[:lane_tiles]
        tall[depth + k * lane_tiles : depth + (k + 1) * lane_tiles, :] = both[lane_tiles:]
    mixer[...] = tall[...].T.astype(BF16)


def place_table(slots, nu_ref, first):
    shell = iota((8, LANE), 1)
    place = jnp.full((8, LANE), slots, I32)
    for k in range(slots):
        here = jnp.where(first[k], nu_ref[0, k], -1)
        turned = jnp.where(shell % 2 == k % 2, k // 2, slots // 2 + k // 2)
        place = jnp.where(shell == here, turned, place)
    return place


def half_transform(slots, occ_count, q, blocks, mixer, spread, prods, ext):
    lane_tiles = SHELL * SHELL // LANE
    depth = slots * lane_tiles
    wide = slots * occ_count

    @pl.loop(0, slots)
    def _(k):
        for t in range(lane_tiles):
            at = pl.multiple_of((k * lane_tiles + t) * ROWS, ROWS)
            spread[pl.ds(at, ROWS), :] = blocks[q, k, :, t * LANE : (t + 1) * LANE].astype(F32)

    left = left_half((depth, LANE))
    for r in range(0, HALF, 2):
        columns = []
        for e in range(2):
            one = spread[pl.ds(r + e, depth, stride=ROWS), :]
            two = spread[pl.ds(r + e + HALF, depth, stride=ROWS), :]
            columns.append(jnp.concatenate(halves_apart(one, two, left), axis=0).astype(BF16))
        both = jnp.dot(mixer[...], jnp.concatenate(columns, axis=1), preferred_element_type=F32)
        for e in range(2):
            prods[(r + e) * wide : (r + e + 1) * wide, :] = both[:, e * LANE : (e + 1) * LANE]

    left = left_half((HALF, LANE))
    for i in range(occ_count + 1):
        batch = (i - 1) % occ_count
        for s in range(slots // 2):
            one = prods[pl.ds(2 * s * occ_count + batch, HALF, stride=wide), :]
            two = prods[pl.ds((2 * s + 1) * occ_count + batch, HALF, stride=wide), :]
            pair = jnp.concatenate(halves_apart(one, two, left), axis=0)
            ext[q, i, :, s * LANE : (s + 1) * LANE] = pair.astype(BF16)


def folded(values):
    rows, cols = values.shape
    if cols % LANE:
        values = jnp.concatenate([values, jnp.zeros((rows, LANE - cols % LANE), F32)], axis=1)
    result = values[:, :LANE]
    for c in range(LANE, values.shape[1], LANE):
        result = result + values[:, c : c + LANE]
    return jnp.sum(result.reshape(rows // 8, 8, LANE), axis=0)


def pair_kernel(
    n_aux,
    n_occ,
    pieces,
    integrals_ref,
    mu_ref,
    nu_ref,
    count_ref,
    occ_ref,
    vir_ref,
    order_ref,
    eocc_ref,
    evir_ref,
    amp_ref,
    energy_ref,
    amp,
    blocks,
    occ,
    tall,
    mixer,
    spread,
    prods,
    ext,
    got,
    meta,
    metas,
    places,
    tiles,
    half_y,
    half_x,
    vir,
    vir_t,
    erow,
    eblock,
    lhs,
    wide,
    own,
    out_ring,
    in_ring,
    out_rest,
    in_rest,
    total_u,
    out_lead,
    in_lead,
    out_tail,
    in_tail,
    ratio_lead,
    ratio_tail,
    part,
    parts,
    local_sem,
    keep_sem,
    meta_send,
    meta_recv,
    data_send,
    data_recv,
    single_send,
    single_recv,
    pass_send,
    pass_recv,
    ring_send,
    ring_recv,
    lead_send,
    lead_recv,
    tail_send,
    tail_recv,
    part_send,
    part_recv,
):
    a = lax.axis_index("aux")
    g = lax.axis_index("occ")
    odd = lax.rem(a, 2)
    chip = a // 2
    mate = a + 1 - 2 * odd
    chips = n_aux // 2
    slots = blocks.shape[1]
    chunks = blocks.shape[0]
    occ_count = occ.shape[0]
    nvir, nu_w = vir.shape
    width = nvir // n_occ
    padded = vir_t.shape[1]
    slab = chunks * ROWS
    packs = slots // 2
    nu_tiles = nu_w // LANE

    def near(step):
        if chips != 16:
            return lax.rem(chip + step + chips, chips)
        return lax.rem(chip // 4 + step // 4, 4) * 4 + lax.rem(chip + step, 4)

    def back(step):
        if chips != 16:
            return lax.rem(chip - step + chips, chips)
        return lax.rem(chip // 4 - step // 4 + 4, 4) * 4 + lax.rem(chip % 4 - step % 4 + 4, 4)

    def around(step):
        return lax.rem(g + step + 2 * n_occ, n_occ)

    loads = [pltpu.make_async_copy(occ_ref, occ, local_sem.at[0])]
    for q in range(chunks):
        loads.append(
            pltpu.make_async_copy(integrals_ref.at[:, pl.ds(q * ROWS, ROWS)], blocks.at[q], local_sem.at[q + 1])
        )
    load_vir = pltpu.make_async_copy(vir_ref, vir, local_sem.at[chunks + 1])
    for load in loads:
        load.start()
    load_vir.start()

    barrier = pltpu.get_barrier_semaphore()

    @pl.loop(1, chips)
    def _(d):
        pl.semaphore_signal(barrier, inc=1, device_id={"aux": 2 * near(d) + odd}, device_id_type=MESH)

    pl.semaphore_signal(barrier, inc=1, device_id={"aux": mate}, device_id_type=MESH)

    @pl.loop(1, n_occ)
    def _(d):
        pl.semaphore_signal(barrier, inc=1, device_id={"occ": around(d)}, device_id_type=MESH)

    live, first = first_of_kind(slots, nu_ref, count_ref[0])
    meta[...] = place_table(slots, nu_ref, first)
    metas[odd, chip] = meta[...]
    loads[0].wait()
    build_mixer(slots, occ_count, mu_ref, nu_ref, order_ref, live, first, occ, tall, mixer)

    def meta_copy(d):
        return pltpu.make_async_remote_copy(
            meta,
            metas.at[odd, chip],
            meta_send.at[d],
            meta_recv.at[d],
            device_id={"aux": 2 * near(d) + odd},
            device_id_type=MESH,
        )

    def meta_pass():
        return pltpu.make_async_remote_copy(
            metas.at[odd], metas.at[odd], meta_send.at[0], meta_recv.at[0], device_id={"aux": mate}, device_id_type=MESH
        )

    def data_copy(q, d):
        to = near(d)
        return pltpu.make_async_remote_copy(
            ext.at[q, pl.ds(2 * to, 2)],
            got.at[odd, chip, q, pl.ds(0, 2)],
            data_send.at[q, d],
            data_recv.at[q, d],
            device_id={"aux": 2 * to + odd},
            device_id_type=MESH,
        )

    def single_copy(parity, d):
        to = near(d)
        return pltpu.make_async_remote_copy(
            ext.at[:, 2 * to + 2],
            got.at[odd, chip, :, 2],
            single_send.at[d],
            single_recv.at[parity, d],
            device_id={"aux": 2 * to + 1},
            device_id_type=MESH,
        )

    def keep_copy(q):
        return pltpu.make_async_copy(ext.at[q, pl.ds(2 * chip, 3)], got.at[odd, chip, q], keep_sem.at[q])

    def pass_copy(d):
        view = got.at[odd, back(d), :, pl.ds(0, 2)]
        return pltpu.make_async_remote_copy(
            view, view, pass_send.at[d], pass_recv.at[d], device_id={"aux": mate}, device_id_type=MESH
        )

    @pl.loop(0, chunks)
    def _(q):
        pltpu.make_async_copy(
            integrals_ref.at[:, pl.ds(pl.multiple_of(q * ROWS, ROWS), ROWS)], blocks.at[q], local_sem.at[q + 1]
        ).wait()
        half_transform(slots, occ_count, q, blocks, mixer, spread, prods, ext)
        keep_copy(q).start()

        @pl.when(q == 0)
        def _():
            pl.semaphore_wait(barrier, chips + n_occ - 1)

            @pl.loop(1, chips)
            def _(d):
                meta_copy(d).start()

        @pl.loop(1, chips)
        def _(d):
            data_copy(q, d).start()

    @pl.loop(1, chips)
    def _(d):
        meta_copy(d).wait_recv()

    meta_pass().start()
    tiles[:, 2 * packs] = jnp.zeros((2, slab, LANE), BF16)
    load_vir.wait()

    def block_vir(c):
        low = c * width // ROWS * ROWS
        high = -(-(c + 1) * width // ROWS) * ROWS
        off = c * width - low
        for w in range(0, nu_w, LANE):
            rows = vir[low:high, w : w + LANE].astype(F32)[off : off + width]
            if padded > width:
                rows = jnp.concatenate([rows, jnp.zeros((padded - width, LANE), F32)], axis=0)
            vir_t[c, :, w : w + LANE] = rows.astype(BF16)

    for c in range(n_occ // 2):
        block_vir(c)
    meta_pass().wait_recv()
    placing = pltpu.make_async_copy(metas, places, local_sem.at[chunks + 2])
    placing.start()
    for c in range(n_occ // 2, n_occ):
        block_vir(c)
    erow[...] = evir_ref[...].reshape(1, nvir)
    for c in range(n_occ):
        eblock[c] = jnp.concatenate(
            [erow[:, c * width : (c + 1) * width], jnp.ones((1, eblock.shape[2] - width), F32)], axis=1
        )

    for q in range(chunks):
        keep_copy(q).wait()
    pass_copy(0).start()
    placing.wait()

    left = left_half((slab, LANE))

    halves = (half_y, half_x)

    def own_or_not(parity):
        return lax.rem(parity + odd, 2)

    def spread_sides(d, parity, sides):
        source = back(d)
        for side, slot in sides:
            for s in range(packs):
                tile = got[parity, source, :, slot, :, s * LANE : (s + 1) * LANE].reshape(slab, LANE)
                tiles[side, s] = tile
                tiles[side, packs + s] = pltpu.roll(tile.astype(F32), SHELL, 1).astype(BF16)
        rows = pl.ds(pl.multiple_of((own_or_not(parity) * chips + d) * slab, ROWS), slab)
        for c in range(nu_tiles):
            one = places[parity, source, 0, 2 * c]
            two = places[parity, source, 0, 2 * c + 1]
            for side, _ in sides:
                halves[side][rows, c * LANE : (c + 1) * LANE] = jnp.where(left, tiles[side, one], tiles[side, two])

    def spread_out(d, parity):
        @pl.when(odd == 0)
        def _():
            spread_sides(d, parity, ((0, 0), (1, 1)))

        @pl.when(odd == 1)
        def _():
            spread_sides(d, parity, ((0, 1),))

    way = 1 - 2 * odd
    whole = out_ring.shape[1]
    front = out_rest.shape[2]
    rest = (whole, padded - whole, 1)

    def times(one, two):
        return lax.dot_general(one, two, NT, preferred_element_type=F32)

    def pick_rows(t):
        for row, rows, sign in pieces + [rest]:
            lhs[row : row + rows, :] = vir_t[around(-sign * way * (t + 1)), row : row + rows, :]

    def column_cuts(step):
        return [(c, min(c + step, nu_w)) for c in range(0, nu_w, step)]

    pick_rows(0)

    group = chips // 2
    group_rows = group * slab

    def rows_of(k):
        return pl.ds(pl.multiple_of(k * group_rows, group_rows), group_rows)

    def add_products(k):
        rows = rows_of(k)

        @pl.when(k == 0)
        def _():
            for low, high in column_cuts(256):
                own[:, low:high] = jnp.dot(wide[:, rows], half_x[rows, low:high], preferred_element_type=F32)

        @pl.when(k > 0)
        def _():
            for low, high in column_cuts(256):
                own[:, low:high] += jnp.dot(wide[:, rows], half_x[rows, low:high], preferred_element_type=F32)

    def widen(k):
        rows = rows_of(k)
        wide[:, rows] = times(lhs[...], half_y[rows, :]).astype(BF16)

        @pl.when(odd == 0)
        def _():
            add_products(k)

    @pl.when(odd == 0)
    def _():
        single_copy(0, 0).start()

    @pl.loop(1, chips)
    def _(d):
        single_copy(odd, d).start()

    @pl.loop(0, 2)
    def _(k):
        @pl.loop(0, group)
        def _(step):
            d = k * group + step

            @pl.when(d > 0)
            def _():
                @pl.loop(0, chunks)
                def _(q):
                    data_copy(q, d).wait_recv()

                pass_copy(d).start()

            spread_out(d, odd)

            @pl.when(k == 1)
            def _():
                pass_copy(step).wait_recv()
                spread_out(step, 1 - odd)

        widen(k)

    widen(2)

    @pl.loop(group, chips)
    def _(d):
        pass_copy(d).wait_recv()
        spread_out(d, 1 - odd)

    widen(3)

    @pl.when(odd == 1)
    def _():
        @pl.loop(0, 2)
        def _(k):
            @pl.loop(0, group)
            def _(step):
                d = k * group + step
                single_copy(0, d).wait_recv()
                spread_sides(d, 0, ((1, 2),))

                @pl.when(d > 0)
                def _():
                    single_copy(1, d).wait_recv()

                spread_sides(d, 1, ((1, 2),))

            add_products(k)
            add_products(k + 2)

    def ring_copy(t, k):
        if k == len(pieces):
            source, target = out_rest.at[t], in_rest.at[t]
            sign = 1
        else:
            row, rows, sign = pieces[k]
            source, target = out_ring.at[t, pl.ds(row, rows)], in_ring.at[t, pl.ds(row, rows)]
        return pltpu.make_async_remote_copy(
            source,
            target,
            ring_send.at[k, t],
            ring_recv.at[k, t],
            device_id={"occ": around(way * sign)},
            device_id_type=MESH,
        )

    def packed_rest():
        back_part = own[whole : whole + 8, front:]
        if back_part.shape[1] < front:
            back_part = jnp.concatenate([back_part, jnp.zeros((8, front - back_part.shape[1]), F32)], axis=1)
        return jnp.concatenate([own[whole : whole + 8, :front], back_part], axis=0)

    @pl.loop(0, n_occ)
    def _(t):
        @pl.when(t > 0)
        def _():
            pick_rows(t)
            for p in range(0, n_aux * slab, 256):
                end = min(p + 256, n_aux * slab)
                wide[:, p:end] = lax.dot_general(
                    lhs[...], half_y[p:end, :], NT, preferred_element_type=F32
                ).astype(BF16)
            for low, high in column_cuts(256):
                own[:, low:high] = jnp.dot(wide[...], half_x[:, low:high], preferred_element_type=F32)

        for k in range(len(pieces) + 1):
            if k < len(pieces):
                span = slice(pieces[k][0], pieces[k][0] + pieces[k][1])

            @pl.when(t == 0)
            def _():
                if k < len(pieces):
                    out_ring[t, span, :] = own[span, :].astype(BF16)
                else:
                    out_rest[t] = packed_rest().astype(BF16)

            @pl.when(t > 0)
            def _():
                ring_copy(t - 1, k).wait_recv()
                if k < len(pieces):
                    out_ring[t, span, :] = (own[span, :] + in_ring[t - 1, span, :].astype(F32)).astype(BF16)
                else:
                    out_rest[t] = (packed_rest() + in_rest[t - 1].astype(F32)).astype(BF16)

            @pl.when(t < n_occ - 1)
            def _():
                ring_copy(t, k).start()

    last = n_occ - 1
    total_u[:whole, :] = out_ring[last]
    packed = out_rest[last].astype(F32)
    unpacked = jnp.concatenate([packed[:8], packed[8:, : nu_w - front]], axis=1)
    total_u[whole:, :] = jnp.concatenate([unpacked, jnp.zeros((padded - whole - 8, nu_w), F32)], axis=0).astype(BF16)

    farthest = n_occ // 2
    far = farthest - 1
    far_block = around(farthest)
    nearer_half = g < farthest

    def tile_step(d):
        return way * (d if d % 2 == 1 else -d)

    def lead_copy(d):
        return pltpu.make_async_remote_copy(
            out_lead.at[d - 1],
            in_lead.at[d - 1],
            lead_send.at[d - 1],
            lead_recv.at[d - 1],
            device_id={"occ": around(tile_step(d))},
            device_id_type=MESH,
        )

    def tail_copy(d):
        return pltpu.make_async_remote_copy(
            out_tail.at[d - 1],
            in_tail.at[d - 1],
            tail_send.at[d - 1],
            tail_recv.at[d - 1],
            device_id={"occ": around(tile_step(d))},
            device_id_type=MESH,
        )

    @pl.when(nearer_half)
    def _():
        out_lead[far] = times(total_u[...], vir_t[far_block, :LANE, :]).astype(BF16)
        lead_copy(farthest).start()

    @pl.when(jnp.logical_not(nearer_half))
    def _():
        out_tail[far] = times(total_u[LANE:, :], vir_t[far_block]).astype(BF16)
        tail_copy(farthest).start()

    for d in range(far, 0, -1):
        to = around(tile_step(d))
        out_lead[d - 1] = times(total_u[...], vir_t[to, :LANE, :]).astype(BF16)
        lead_copy(d).start()
        out_tail[d - 1] = times(vir_t[to, LANE:, :], total_u[...]).astype(BF16)
        tail_copy(d).start()

    e_pair = eocc_ref[order_ref[a]] + eocc_ref[order_ref[lax.rem(a + n_aux - 1, n_aux)]]

    def e_row(h, low, high):
        return eblock[h][:, low:high]

    def e_column(h, low, high):
        return jnp.broadcast_to(eblock[h], (8, eblock.shape[2])).T[low:high, 0:1]

    e_rows = e_pair - e_column(g, 0, padded)
    total = jnp.zeros((8, LANE), F32)
    for c in range(0, nvir, 256):
        end = min(c + 256, nvir)
        pair = times(total_u[...], vir[c:end, :])
        ratio = pair / (e_rows - erow[:, c:end])
        amp[0, :, c:end] = ratio[:width].astype(BF16)
        total = total + folded(ratio * (2.0 * pair))
    leaving = pltpu.make_async_copy(amp, amp_ref, local_sem.at[0])
    leaving.start()

    block = times(total_u[...], vir_t[g])
    same = times(vir_t[g], total_u[...])
    total = total - folded(block / (e_rows - e_row(g, 0, padded)) * same)

    def lead_ratio(h):
        under = (e_pair - e_column(h, 0, padded)) - e_row(g, 0, LANE)
        return times(vir_t[h], total_u[:LANE, :]) / under

    for d in range(1, farthest):
        source = around(-tile_step(d))
        ratio_lead[d - 1] = lead_ratio(source)
        ratio_tail[d - 1] = times(total_u[LANE:, :], vir_t[source]) / (e_rows[LANE:] - e_row(source, 0, padded))

    @pl.when(nearer_half)
    def _():
        under = (e_pair - e_column(far_block, LANE, padded)) - e_row(g, 0, padded)
        ratio_tail[far] = times(vir_t[far_block, LANE:, :], total_u[...]) / under

    @pl.when(jnp.logical_not(nearer_half))
    def _():
        ratio_lead[far] = lead_ratio(far_block)

    part[...] = total
    for d in range(1, farthest):
        lead_copy(d).wait_recv()
        tail_copy(d).wait_recv()
        met = folded(ratio_lead[d - 1] * in_lead[d - 1].astype(F32))
        part[...] -= 2.0 * (met + folded(ratio_tail[d - 1] * in_tail[d - 1].astype(F32)))

    @pl.when(nearer_half)
    def _():
        tail_copy(farthest).wait_recv()
        part[...] -= 2.0 * folded(ratio_tail[far] * in_tail[far].astype(F32))

    @pl.when(jnp.logical_not(nearer_half))
    def _():
        lead_copy(farthest).wait_recv()
        part[...] -= 2.0 * folded(ratio_lead[far] * in_lead[far].astype(F32))

    total = part[...]

    def part_copy(d):
        return pltpu.make_async_remote_copy(
            part, parts.at[d], part_send.at[d], part_recv.at[d], device_id={"occ": around(d)}, device_id_type=MESH
        )

    for d in sorted(range(1, n_occ), key=lambda d: -min(d, n_occ - d)):
        part_copy(d).start()
    for d in range(1, n_occ):
        part_copy(d).wait_recv()
        total = total + parts[d]
    energy_ref[0] = jnp.sum(total) / (nvir * nvir)

    leaving.wait()
    for d in range(1, n_occ):
        part_copy(d).wait_send()
    for d in range(1, farthest):
        lead_copy(d).wait_send()
        tail_copy(d).wait_send()

    @pl.when(nearer_half)
    def _():
        lead_copy(farthest).wait_send()

    @pl.when(jnp.logical_not(nearer_half))
    def _():
        tail_copy(farthest).wait_send()

    @pl.loop(0, n_occ - 1)
    def _(t):
        for k in range(len(pieces) + 1):
            ring_copy(t, k).wait_send()

    meta_pass().wait_send()

    @pl.loop(1, chips)
    def _(d):
        meta_copy(d).wait_send()

    @pl.loop(0, chunks)
    def _(q):
        @pl.loop(1, chips)
        def _(d):
            data_copy(q, d).wait_send()

    @pl.loop(0, chips)
    def _(d):
        pass_copy(d).wait_send()

    @pl.when(odd == 0)
    def _():
        single_copy(0, 0).wait_send()

    @pl.loop(1, chips)
    def _(d):
        single_copy(odd, d).wait_send()


def pair_results(
    n_aux, n_occ, integrals, mu_shells, nu_shells, block_count, occ_t, vir_t, occ_order, occ_energies, vir_energies
):
    slots, slab, _ = integrals.shape
    occ_count, nao = occ_t.shape
    nvir, nu_w = vir_t.shape
    width = nvir // n_occ
    padded = -(-width // ROWS) * ROWS
    chunks = slab // ROWS
    chips = n_aux // 2
    aux_rows = n_aux * slab
    farthest = n_occ // 2
    spread_rows = slots * SHELL * SHELL // LANE * ROWS
    mixed = slots * occ_count
    whole = width // ROWS * ROWS
    front = -(-nu_w // (2 * LANE)) * LANE
    middle = whole // (2 * ROWS) * ROWS
    step = 32
    ahead = [(row, min(step, middle - row), 1) for row in range(0, middle, step)]
    behind = [(row, min(step, whole - row), -1) for row in range(middle, whole, step)]
    pieces = [piece for both in zip(ahead, behind) for piece in both]
    vmem = pl.BlockSpec(memory_space=pltpu.VMEM)
    smem = pl.BlockSpec(memory_space=pltpu.SMEM)
    anywhere = pl.BlockSpec(memory_space=pl.ANY)
    dma = pltpu.SemaphoreType.DMA
    macs = 2 * n_occ * padded * aux_rows * nu_w
    return pl.pallas_call(
        functools.partial(pair_kernel, n_aux, n_occ, pieces),
        in_specs=[anywhere, smem, smem, smem, anywhere, anywhere, smem, smem, vmem],
        out_specs=(anywhere, smem),
        out_shape=(jax.ShapeDtypeStruct((1, width, nvir), BF16), jax.ShapeDtypeStruct((1,), F32)),
        scratch_shapes=[
            pltpu.VMEM((1, width, nvir), BF16),
            pltpu.VMEM((chunks, slots, ROWS, SHELL * SHELL), BF16),
            pltpu.VMEM((occ_count, nao), BF16),
            pltpu.VMEM((slots * SHELL, mixed), F32),
            pltpu.VMEM((mixed, slots * SHELL), BF16),
            pltpu.VMEM((spread_rows, LANE), F32),
            pltpu.VMEM((HALF * mixed, LANE), F32),
            pltpu.VMEM((chunks, occ_count + 1, ROWS, slots * SHELL), BF16),
            pltpu.VMEM((2, chips, chunks, 3, ROWS, slots * SHELL), BF16),
            pltpu.VMEM((8, LANE), I32),
            pltpu.VMEM((2, chips, 8, LANE), I32),
            pltpu.SMEM((2, chips, 8, LANE), I32),
            pltpu.VMEM((2, slots + 1, slab, LANE), BF16),
            pltpu.VMEM((aux_rows, nu_w), BF16),
            pltpu.VMEM((aux_rows, nu_w), BF16),
            pltpu.VMEM((nvir, nu_w), BF16),
            pltpu.VMEM((n_occ, padded, nu_w), BF16),
            pltpu.VMEM((1, nvir), F32),
            pltpu.VMEM((n_occ, 1, -(-padded // LANE) * LANE), F32),
            pltpu.VMEM((padded, nu_w), BF16),
            pltpu.VMEM((padded, aux_rows), BF16),
            pltpu.VMEM((padded, nu_w), F32),
            pltpu.VMEM((n_occ, whole, nu_w), BF16),
            pltpu.VMEM((n_occ - 1, whole, nu_w), BF16),
            pltpu.VMEM((n_occ, ROWS, front), BF16),
            pltpu.VMEM((n_occ - 1, ROWS, front), BF16),
            pltpu.VMEM((padded, nu_w), BF16),
            pltpu.VMEM((farthest, padded, LANE), BF16),
            pltpu.VMEM((farthest, padded, LANE), BF16),
            pltpu.VMEM((farthest, padded - LANE, padded), BF16),
            pltpu.VMEM((farthest, padded - LANE, padded), BF16),
            pltpu.VMEM((farthest, padded, LANE), F32),
            pltpu.VMEM((farthest, padded - LANE, padded), F32),
            pltpu.VMEM((8, LANE), F32),
            pltpu.VMEM((n_occ, 8, LANE), F32),
            dma((chunks + 3,)),
            dma((chunks,)),
            dma((chips,)),
            dma((chips,)),
            dma((chunks, chips)),
            dma((chunks, chips)),
            dma((chips,)),
            dma((2, chips)),
            dma((chips,)),
            dma((chips,)),
            dma((len(pieces) + 1, n_occ - 1)),
            dma((len(pieces) + 1, n_occ - 1)),
            dma((farthest,)),
            dma((farthest,)),
            dma((farthest,)),
            dma((farthest,)),
            dma((n_occ,)),
            dma((n_occ,)),
        ],
        compiler_params=pltpu.CompilerParams(
            collective_id=0, has_side_effects=True, vmem_limit_bytes=60 * 2**20
        ),
        cost_estimate=pl.CostEstimate(flops=2 * macs, bytes_accessed=2 * nu_w * nvir, transcendentals=0),
    )(integrals, mu_shells, nu_shells, block_count, occ_t, vir_t, occ_order, occ_energies, vir_energies)


def local(
    n_aux,
    n_occ,
    integrals,
    mu_shells,
    nu_shells,
    block_count,
    occ_coeffs,
    vir_coeffs,
    occ_order,
    occ_energies,
    vir_energies,
):
    return pair_results(
        n_aux,
        n_occ,
        integrals[0],
        mu_shells,
        nu_shells,
        block_count,
        occ_coeffs.T,
        vir_coeffs.T,
        occ_order,
        occ_energies,
        vir_energies,
    )


def solution(mesh):
    placed = (
        P(("aux", "occ"), None, None, None),
        P(("aux", "occ"), None),
        P(("aux", "occ"), None),
        P(("aux", "occ")),
        P(),
        P(),
        P(),
        P(),
        P(),
    )
    return jax.shard_map(
        functools.partial(local, mesh.shape["aux"], mesh.shape["occ"]),
        mesh=mesh,
        in_specs=placed,
        out_specs=(P("aux", "occ", None), P("aux")),
        check_vma=False,
    )
```

```python
import functools

import jax
import jax.numpy as jnp
from jax import lax
from jax.experimental import pallas as pl
from jax.experimental.pallas import tpu as pltpu
from jax.sharding import PartitionSpec as P

SHELL = 64
LANE = 128
ROWS = 16
HALF = ROWS // 2
MESH = pl.DeviceIdType.MESH
F32 = jnp.float32
BF16 = jnp.bfloat16
I32 = jnp.int32
NT = (((1,), (1,)), ((), ()))


def left_half(shape):
    return lax.broadcasted_iota(I32, shape, len(shape) - 1) < SHELL


def iota(shape, dim):
    return lax.broadcasted_iota(I32, shape, dim)


def halves_apart(one, two, left):
    turned = pltpu.roll(jnp.where(left, two, one), SHELL, 1)
    return [jnp.where(left, one, turned), jnp.where(left, turned, two)]


def first_of_kind(slots, nu_ref, count):
    live = [k < count for k in range(slots)]
    first = []
    for k in range(slots):
        new = live[k]
        for j in range(k):
            new = new & (nu_ref[0, j] != nu_ref[0, k])
        first.append(new)
    return live, first


def build_mixer(slots, occ_count, mu_ref, nu_ref, order_ref, live, first, occ, tall, mixer):
    lane_tiles = SHELL * SHELL // LANE
    depth = slots * lane_tiles
    wide = slots * occ_count
    lane = iota((1, wide), 1)
    batch = lane % occ_count
    target = lane // occ_count
    order = jnp.zeros((1, wide), I32)
    for i in range(occ_count):
        order = jnp.where(batch == i, order_ref[i], order)
    shell = jnp.full((1, wide), -1, I32)
    for k in range(slots):
        shell = jnp.where(target == k, jnp.where(first[k], nu_ref[0, k], -1), shell)
    picked = iota((occ_count, wide), 0) == order
    row = iota((SHELL, LANE), 0)
    col = iota((SHELL, LANE), 1)
    wanted = 2 * (row % lane_tiles) + row // lane_tiles
    for k in range(slots):
        mu = mu_ref[0, k]
        rows = occ[:, :LANE]
        for t in range(1, occ.shape[1] // LANE):
            rows = jnp.where(mu // 2 == t, occ[:, t * LANE : (t + 1) * LANE], rows)
        split = (col == wanted + mu % 2 * SHELL).astype(F32).astype(BF16)
        parted = lax.dot_general(split, rows, NT, preferred_element_type=F32).astype(BF16)
        here = jnp.where(live[k], nu_ref[0, k], -2)
        picker = (picked & (shell == here)).astype(F32).astype(BF16)
        both = jnp.dot(parted, picker, preferred_element_type=F32)
        tall[k * lane_tiles : (k + 1) * lane_tiles, :] = both[:lane_tiles]
        tall[depth + k * lane_tiles : depth + (k + 1) * lane_tiles, :] = both[lane_tiles:]
    mixer[...] = tall[...].T.astype(BF16)


def place_table(slots, nu_ref, first):
    shell = iota((8, LANE), 1)
    place = jnp.full((8, LANE), slots, I32)
    for k in range(slots):
        here = jnp.where(first[k], nu_ref[0, k], -1)
        turned = jnp.where(shell % 2 == k % 2, k // 2, slots // 2 + k // 2)
        place = jnp.where(shell == here, turned, place)
    return place


def half_transform(slots, occ_count, q, blocks, mixer, spread, prods, ext):
    lane_tiles = SHELL * SHELL // LANE
    depth = slots * lane_tiles
    wide = slots * occ_count

    @pl.loop(0, slots)
    def _(k):
        for t in range(lane_tiles):
            at = pl.multiple_of((k * lane_tiles + t) * ROWS, ROWS)
            spread[pl.ds(at, ROWS), :] = blocks[q, k, :, t * LANE : (t + 1) * LANE].astype(F32)

    left = left_half((depth, LANE))
    for r in range(0, HALF, 2):
        columns = []
        for e in range(2):
            one = spread[pl.ds(r + e, depth, stride=ROWS), :]
            two = spread[pl.ds(r + e + HALF, depth, stride=ROWS), :]
            columns.append(jnp.concatenate(halves_apart(one, two, left), axis=0).astype(BF16))
        both = jnp.dot(mixer[...], jnp.concatenate(columns, axis=1), preferred_element_type=F32)
        for e in range(2):
            prods[(r + e) * wide : (r + e + 1) * wide, :] = both[:, e * LANE : (e + 1) * LANE]

    left = left_half((HALF, LANE))
    for i in range(occ_count + 1):
        batch = (i - 1) % occ_count
        for s in range(slots // 2):
            one = prods[pl.ds(2 * s * occ_count + batch, HALF, stride=wide), :]
            two = prods[pl.ds((2 * s + 1) * occ_count + batch, HALF, stride=wide), :]
            pair = jnp.concatenate(halves_apart(one, two, left), axis=0)
            ext[q, i, :, s * LANE : (s + 1) * LANE] = pair.astype(BF16)


def folded(values):
    rows, cols = values.shape
    if cols % LANE:
        values = jnp.concatenate([values, jnp.zeros((rows, LANE - cols % LANE), F32)], axis=1)
    result = values[:, :LANE]
    for c in range(LANE, values.shape[1], LANE):
        result = result + values[:, c : c + LANE]
    return jnp.sum(result.reshape(rows // 8, 8, LANE), axis=0)


def pair_kernel(
    n_aux,
    n_occ,
    pieces,
    integrals_ref,
    mu_ref,
    nu_ref,
    count_ref,
    occ_ref,
    vir_ref,
    order_ref,
    eocc_ref,
    evir_ref,
    amp_ref,
    energy_ref,
    amp,
    blocks,
    occ,
    tall,
    mixer,
    spread,
    prods,
    ext,
    got,
    meta,
    metas,
    places,
    tiles,
    half_y,
    half_x,
    vir,
    vir_t,
    erow,
    eblock,
    lhs,
    wide,
    own,
    out_ring,
    in_ring,
    out_rest,
    in_rest,
    total_u,
    out_lead,
    in_lead,
    out_tail,
    in_tail,
    ratio_lead,
    ratio_tail,
    part,
    parts,
    local_sem,
    keep_sem,
    meta_send,
    meta_recv,
    data_send,
    data_recv,
    single_send,
    single_recv,
    pass_send,
    pass_recv,
    ring_send,
    ring_recv,
    lead_send,
    lead_recv,
    tail_send,
    tail_recv,
    part_send,
    part_recv,
):
    a = lax.axis_index("aux")
    g = lax.axis_index("occ")
    odd = lax.rem(a, 2)
    chip = a // 2
    mate = a + 1 - 2 * odd
    chips = n_aux // 2
    slots = blocks.shape[1]
    chunks = blocks.shape[0]
    occ_count = occ.shape[0]
    nvir, nu_w = vir.shape
    width = nvir // n_occ
    padded = vir_t.shape[1]
    slab = chunks * ROWS
    packs = slots // 2
    nu_tiles = nu_w // LANE

    def near(step):
        if chips != 16:
            return lax.rem(chip + step + chips, chips)
        return lax.rem(chip // 4 + step // 4, 4) * 4 + lax.rem(chip + step, 4)

    def back(step):
        if chips != 16:
            return lax.rem(chip - step + chips, chips)
        return lax.rem(chip // 4 - step // 4 + 4, 4) * 4 + lax.rem(chip % 4 - step % 4 + 4, 4)

    def around(step):
        return lax.rem(g + step + 2 * n_occ, n_occ)

    loads = [pltpu.make_async_copy(occ_ref, occ, local_sem.at[0])]
    for q in range(chunks):
        loads.append(
            pltpu.make_async_copy(integrals_ref.at[:, pl.ds(q * ROWS, ROWS)], blocks.at[q], local_sem.at[q + 1])
        )
    load_vir = pltpu.make_async_copy(vir_ref, vir, local_sem.at[chunks + 1])
    for load in loads:
        load.start()
    load_vir.start()

    barrier = pltpu.get_barrier_semaphore()

    @pl.loop(1, chips)
    def _(d):
        pl.semaphore_signal(barrier, inc=1, device_id={"aux": 2 * near(d) + odd}, device_id_type=MESH)

    pl.semaphore_signal(barrier, inc=1, device_id={"aux": mate}, device_id_type=MESH)

    @pl.loop(1, n_occ)
    def _(d):
        pl.semaphore_signal(barrier, inc=1, device_id={"occ": around(d)}, device_id_type=MESH)

    live, first = first_of_kind(slots, nu_ref, count_ref[0])
    meta[...] = place_table(slots, nu_ref, first)
    metas[odd, chip] = meta[...]
    loads[0].wait()
    build_mixer(slots, occ_count, mu_ref, nu_ref, order_ref, live, first, occ, tall, mixer)

    def meta_copy(d):
        return pltpu.make_async_remote_copy(
            meta,
            metas.at[odd, chip],
            meta_send.at[d],
            meta_recv.at[d],
            device_id={"aux": 2 * near(d) + odd},
            device_id_type=MESH,
        )

    def meta_pass():
        return pltpu.make_async_remote_copy(
            metas.at[odd], metas.at[odd], meta_send.at[0], meta_recv.at[0], device_id={"aux": mate}, device_id_type=MESH
        )

    def data_copy(q, d):
        to = near(d)
        return pltpu.make_async_remote_copy(
            ext.at[q, pl.ds(2 * to, 2)],
            got.at[odd, chip, q, pl.ds(0, 2)],
            data_send.at[q, d],
            data_recv.at[q, d],
            device_id={"aux": 2 * to + odd},
            device_id_type=MESH,
        )

    def single_copy(parity, d):
        to = near(d)
        return pltpu.make_async_remote_copy(
            ext.at[:, 2 * to + 2],
            got.at[odd, chip, :, 2],
            single_send.at[d],
            single_recv.at[parity, d],
            device_id={"aux": 2 * to + 1},
            device_id_type=MESH,
        )

    def keep_copy(q):
        return pltpu.make_async_copy(ext.at[q, pl.ds(2 * chip, 3)], got.at[odd, chip, q], keep_sem.at[q])

    def pass_copy(d):
        view = got.at[odd, back(d), :, pl.ds(0, 2)]
        return pltpu.make_async_remote_copy(
            view, view, pass_send.at[d], pass_recv.at[d], device_id={"aux": mate}, device_id_type=MESH
        )

    @pl.loop(0, chunks)
    def _(q):
        pltpu.make_async_copy(
            integrals_ref.at[:, pl.ds(pl.multiple_of(q * ROWS, ROWS), ROWS)], blocks.at[q], local_sem.at[q + 1]
        ).wait()
        half_transform(slots, occ_count, q, blocks, mixer, spread, prods, ext)
        keep_copy(q).start()

        @pl.when(q == 0)
        def _():
            pl.semaphore_wait(barrier, chips + n_occ - 1)

            @pl.loop(1, chips)
            def _(d):
                meta_copy(d).start()

        @pl.loop(1, chips)
        def _(d):
            data_copy(q, d).start()

    @pl.loop(1, chips)
    def _(d):
        meta_copy(d).wait_recv()

    meta_pass().start()
    tiles[:, 2 * packs] = jnp.zeros((2, slab, LANE), BF16)
    load_vir.wait()

    def block_vir(c):
        low = c * width // ROWS * ROWS
        high = -(-(c + 1) * width // ROWS) * ROWS
        off = c * width - low
        for w in range(0, nu_w, LANE):
            rows = vir[low:high, w : w + LANE].astype(F32)[off : off + width]
            if padded > width:
                rows = jnp.concatenate([rows, jnp.zeros((padded - width, LANE), F32)], axis=0)
            vir_t[c, :, w : w + LANE] = rows.astype(BF16)

    for c in range(n_occ // 2):
        block_vir(c)
    meta_pass().wait_recv()
    placing = pltpu.make_async_copy(metas, places, local_sem.at[chunks + 2])
    placing.start()
    for c in range(n_occ // 2, n_occ):
        block_vir(c)
    erow[...] = evir_ref[...].reshape(1, nvir)
    for c in range(n_occ):
        eblock[c] = jnp.concatenate(
            [erow[:, c * width : (c + 1) * width], jnp.ones((1, eblock.shape[2] - width), F32)], axis=1
        )

    for q in range(chunks):
        keep_copy(q).wait()
    pass_copy(0).start()
    placing.wait()

    left = left_half((slab, LANE))

    halves = (half_y, half_x)

    def own_or_not(parity):
        return lax.rem(parity + odd, 2)

    def spread_sides(d, parity, sides):
        source = back(d)
        for side, slot in sides:
            for s in range(packs):
                tile = got[parity, source, :, slot, :, s * LANE : (s + 1) * LANE].reshape(slab, LANE)
                tiles[side, s] = tile
                tiles[side, packs + s] = pltpu.roll(tile.astype(F32), SHELL, 1).astype(BF16)
        rows = pl.ds(pl.multiple_of((own_or_not(parity) * chips + d) * slab, ROWS), slab)
        for c in range(nu_tiles):
            one = places[parity, source, 0, 2 * c]
            two = places[parity, source, 0, 2 * c + 1]
            for side, _ in sides:
                halves[side][rows, c * LANE : (c + 1) * LANE] = jnp.where(left, tiles[side, one], tiles[side, two])

    def spread_out(d, parity):
        @pl.when(odd == 0)
        def _():
            spread_sides(d, parity, ((0, 0), (1, 1)))

        @pl.when(odd == 1)
        def _():
            spread_sides(d, parity, ((0, 1),))

    way = 1 - 2 * odd
    whole = out_ring.shape[1]
    front = out_rest.shape[2]
    rest = (whole, padded - whole, 1)

    def times(one, two):
        return lax.dot_general(one, two, NT, preferred_element_type=F32)

    def pick_rows(t):
        for row, rows, sign in pieces + [rest]:
            lhs[row : row + rows, :] = vir_t[around(-sign * way * (t + 1)), row : row + rows, :]

    def column_cuts(step):
        return [(c, min(c + step, nu_w)) for c in range(0, nu_w, step)]

    pick_rows(0)

    group = chips // 2
    group_rows = group * slab

    def rows_of(k):
        return pl.ds(pl.multiple_of(k * group_rows, group_rows), group_rows)

    def add_products(k):
        rows = rows_of(k)

        @pl.when(k == 0)
        def _():
            for low, high in column_cuts(256):
                own[:, low:high] = jnp.dot(wide[:, rows], half_x[rows, low:high], preferred_element_type=F32)

        @pl.when(k > 0)
        def _():
            for low, high in column_cuts(256):
                own[:, low:high] += jnp.dot(wide[:, rows], half_x[rows, low:high], preferred_element_type=F32)

    def widen(k):
        rows = rows_of(k)
        wide[:, rows] = times(lhs[...], half_y[rows, :]).astype(BF16)

        @pl.when(odd == 0)
        def _():
            add_products(k)

    @pl.when(odd == 0)
    def _():
        single_copy(0, 0).start()

    @pl.loop(1, chips)
    def _(d):
        single_copy(odd, d).start()

    @pl.loop(0, 2)
    def _(k):
        @pl.loop(0, group)
        def _(step):
            d = k * group + step

            @pl.when(d > 0)
            def _():
                @pl.loop(0, chunks)
                def _(q):
                    data_copy(q, d).wait_recv()

                pass_copy(d).start()

            spread_out(d, odd)

            @pl.when(k == 1)
            def _():
                pass_copy(step).wait_recv()
                spread_out(step, 1 - odd)

        widen(k)

    widen(2)

    @pl.loop(group, chips)
    def _(d):
        pass_copy(d).wait_recv()
        spread_out(d, 1 - odd)

    widen(3)

    @pl.when(odd == 1)
    def _():
        @pl.loop(0, 2)
        def _(k):
            @pl.loop(0, group)
            def _(step):
                d = k * group + step
                single_copy(0, d).wait_recv()
                spread_sides(d, 0, ((1, 2),))

                @pl.when(d > 0)
                def _():
                    single_copy(1, d).wait_recv()

                spread_sides(d, 1, ((1, 2),))

            add_products(k)
            add_products(k + 2)

    def ring_copy(t, k):
        if k == len(pieces):
            source, target = out_rest.at[t], in_rest.at[t]
            sign = 1
        else:
            row, rows, sign = pieces[k]
            source, target = out_ring.at[t, pl.ds(row, rows)], in_ring.at[t, pl.ds(row, rows)]
        return pltpu.make_async_remote_copy(
            source,
            target,
            ring_send.at[k, t],
            ring_recv.at[k, t],
            device_id={"occ": around(way * sign)},
            device_id_type=MESH,
        )

    def packed_rest():
        back_part = own[whole : whole + 8, front:]
        if back_part.shape[1] < front:
            back_part = jnp.concatenate([back_part, jnp.zeros((8, front - back_part.shape[1]), F32)], axis=1)
        return jnp.concatenate([own[whole : whole + 8, :front], back_part], axis=0)

    @pl.loop(0, n_occ)
    def _(t):
        @pl.when(t > 0)
        def _():
            pick_rows(t)
            for p in range(0, n_aux * slab, 256):
                end = min(p + 256, n_aux * slab)
                wide[:, p:end] = lax.dot_general(
                    lhs[...], half_y[p:end, :], NT, preferred_element_type=F32
                ).astype(BF16)
            for low, high in column_cuts(256):
                own[:, low:high] = jnp.dot(wide[...], half_x[:, low:high], preferred_element_type=F32)

        for k in range(len(pieces) + 1):
            if k < len(pieces):
                span = slice(pieces[k][0], pieces[k][0] + pieces[k][1])

            @pl.when(t == 0)
            def _():
                if k < len(pieces):
                    out_ring[t, span, :] = own[span, :].astype(BF16)
                else:
                    out_rest[t] = packed_rest().astype(BF16)

            @pl.when(t > 0)
            def _():
                ring_copy(t - 1, k).wait_recv()
                if k < len(pieces):
                    out_ring[t, span, :] = (own[span, :] + in_ring[t - 1, span, :].astype(F32)).astype(BF16)
                else:
                    out_rest[t] = (packed_rest() + in_rest[t - 1].astype(F32)).astype(BF16)

            @pl.when(t < n_occ - 1)
            def _():
                ring_copy(t, k).start()

    last = n_occ - 1
    total_u[:whole, :] = out_ring[last]
    packed = out_rest[last].astype(F32)
    unpacked = jnp.concatenate([packed[:8], packed[8:, : nu_w - front]], axis=1)
    total_u[whole:, :] = jnp.concatenate([unpacked, jnp.zeros((padded - whole - 8, nu_w), F32)], axis=0).astype(BF16)

    farthest = n_occ // 2
    far = farthest - 1
    far_block = around(farthest)
    nearer_half = g < farthest

    def tile_step(d):
        return way * (d if d % 2 == 1 else -d)

    def lead_copy(d):
        return pltpu.make_async_remote_copy(
            out_lead.at[d - 1],
            in_lead.at[d - 1],
            lead_send.at[d - 1],
            lead_recv.at[d - 1],
            device_id={"occ": around(tile_step(d))},
            device_id_type=MESH,
        )

    def tail_copy(d):
        return pltpu.make_async_remote_copy(
            out_tail.at[d - 1],
            in_tail.at[d - 1],
            tail_send.at[d - 1],
            tail_recv.at[d - 1],
            device_id={"occ": around(tile_step(d))},
            device_id_type=MESH,
        )

    @pl.when(nearer_half)
    def _():
        out_lead[far] = times(total_u[...], vir_t[far_block, :LANE, :]).astype(BF16)
        lead_copy(farthest).start()

    @pl.when(jnp.logical_not(nearer_half))
    def _():
        out_tail[far] = times(total_u[LANE:, :], vir_t[far_block]).astype(BF16)
        tail_copy(farthest).start()

    for d in range(far, 0, -1):
        to = around(tile_step(d))
        out_lead[d - 1] = times(total_u[...], vir_t[to, :LANE, :]).astype(BF16)
        lead_copy(d).start()
        out_tail[d - 1] = times(vir_t[to, LANE:, :], total_u[...]).astype(BF16)
        tail_copy(d).start()

    e_pair = eocc_ref[order_ref[a]] + eocc_ref[order_ref[lax.rem(a + n_aux - 1, n_aux)]]

    def e_row(h, low, high):
        return eblock[h][:, low:high]

    def e_column(h, low, high):
        return jnp.broadcast_to(eblock[h], (8, eblock.shape[2])).T[low:high, 0:1]

    e_rows = e_pair - e_column(g, 0, padded)
    total = jnp.zeros((8, LANE), F32)
    for c in range(0, nvir, 256):
        end = min(c + 256, nvir)
        pair = times(total_u[...], vir[c:end, :])
        ratio = pair / (e_rows - erow[:, c:end])
        amp[0, :, c:end] = ratio[:width].astype(BF16)
        total = total + folded(ratio * (2.0 * pair))
    leaving = pltpu.make_async_copy(amp, amp_ref, local_sem.at[0])
    leaving.start()

    block = times(total_u[...], vir_t[g])
    same = times(vir_t[g], total_u[...])
    total = total - folded(block / (e_rows - e_row(g, 0, padded)) * same)

    def lead_ratio(h):
        under = (e_pair - e_column(h, 0, padded)) - e_row(g, 0, LANE)
        return times(vir_t[h], total_u[:LANE, :]) / under

    for d in range(1, farthest):
        source = around(-tile_step(d))
        ratio_lead[d - 1] = lead_ratio(source)
        ratio_tail[d - 1] = times(total_u[LANE:, :], vir_t[source]) / (e_rows[LANE:] - e_row(source, 0, padded))

    @pl.when(nearer_half)
    def _():
        under = (e_pair - e_column(far_block, LANE, padded)) - e_row(g, 0, padded)
        ratio_tail[far] = times(vir_t[far_block, LANE:, :], total_u[...]) / under

    @pl.when(jnp.logical_not(nearer_half))
    def _():
        ratio_lead[far] = lead_ratio(far_block)

    part[...] = total
    for d in range(1, farthest):
        lead_copy(d).wait_recv()
        tail_copy(d).wait_recv()
        met = folded(ratio_lead[d - 1] * in_lead[d - 1].astype(F32))
        part[...] -= 2.0 * (met + folded(ratio_tail[d - 1] * in_tail[d - 1].astype(F32)))

    @pl.when(nearer_half)
    def _():
        tail_copy(farthest).wait_recv()
        part[...] -= 2.0 * folded(ratio_tail[far] * in_tail[far].astype(F32))

    @pl.when(jnp.logical_not(nearer_half))
    def _():
        lead_copy(farthest).wait_recv()
        part[...] -= 2.0 * folded(ratio_lead[far] * in_lead[far].astype(F32))

    total = part[...]

    def part_copy(d):
        return pltpu.make_async_remote_copy(
            part, parts.at[d], part_send.at[d], part_recv.at[d], device_id={"occ": around(d)}, device_id_type=MESH
        )

    for d in sorted(range(1, n_occ), key=lambda d: -min(d, n_occ - d)):
        part_copy(d).start()
    for d in range(1, n_occ):
        part_copy(d).wait_recv()
        total = total + parts[d]
    energy_ref[0] = jnp.sum(total) / (nvir * nvir)

    leaving.wait()
    for d in range(1, n_occ):
        part_copy(d).wait_send()
    for d in range(1, farthest):
        lead_copy(d).wait_send()
        tail_copy(d).wait_send()

    @pl.when(nearer_half)
    def _():
        lead_copy(farthest).wait_send()

    @pl.when(jnp.logical_not(nearer_half))
    def _():
        tail_copy(farthest).wait_send()

    @pl.loop(0, n_occ - 1)
    def _(t):
        for k in range(len(pieces) + 1):
            ring_copy(t, k).wait_send()

    meta_pass().wait_send()

    @pl.loop(1, chips)
    def _(d):
        meta_copy(d).wait_send()

    @pl.loop(0, chunks)
    def _(q):
        @pl.loop(1, chips)
        def _(d):
            data_copy(q, d).wait_send()

    @pl.loop(0, chips)
    def _(d):
        pass_copy(d).wait_send()

    @pl.when(odd == 0)
    def _():
        single_copy(0, 0).wait_send()

    @pl.loop(1, chips)
    def _(d):
        single_copy(odd, d).wait_send()


def pair_results(
    n_aux, n_occ, integrals, mu_shells, nu_shells, block_count, occ_t, vir_t, occ_order, occ_energies, vir_energies
):
    slots, slab, _ = integrals.shape
    occ_count, nao = occ_t.shape
    nvir, nu_w = vir_t.shape
    width = nvir // n_occ
    padded = -(-width // ROWS) * ROWS
    chunks = slab // ROWS
    chips = n_aux // 2
    aux_rows = n_aux * slab
    farthest = n_occ // 2
    spread_rows = slots * SHELL * SHELL // LANE * ROWS
    mixed = slots * occ_count
    whole = width // ROWS * ROWS
    front = -(-nu_w // (2 * LANE)) * LANE
    middle = whole // (2 * ROWS) * ROWS
    step = 48
    ahead = [(row, min(step, middle - row), 1) for row in range(0, middle, step)]
    behind = [(row, min(step, whole - row), -1) for row in range(middle, whole, step)]
    pieces = [piece for both in zip(ahead, behind) for piece in both]
    vmem = pl.BlockSpec(memory_space=pltpu.VMEM)
    smem = pl.BlockSpec(memory_space=pltpu.SMEM)
    anywhere = pl.BlockSpec(memory_space=pl.ANY)
    dma = pltpu.SemaphoreType.DMA
    macs = 2 * n_occ * padded * aux_rows * nu_w
    return pl.pallas_call(
        functools.partial(pair_kernel, n_aux, n_occ, pieces),
        in_specs=[anywhere, smem, smem, smem, anywhere, anywhere, smem, smem, vmem],
        out_specs=(anywhere, smem),
        out_shape=(jax.ShapeDtypeStruct((1, width, nvir), BF16), jax.ShapeDtypeStruct((1,), F32)),
        scratch_shapes=[
            pltpu.VMEM((1, width, nvir), BF16),
            pltpu.VMEM((chunks, slots, ROWS, SHELL * SHELL), BF16),
            pltpu.VMEM((occ_count, nao), BF16),
            pltpu.VMEM((slots * SHELL, mixed), F32),
            pltpu.VMEM((mixed, slots * SHELL), BF16),
            pltpu.VMEM((spread_rows, LANE), F32),
            pltpu.VMEM((HALF * mixed, LANE), F32),
            pltpu.VMEM((chunks, occ_count + 1, ROWS, slots * SHELL), BF16),
            pltpu.VMEM((2, chips, chunks, 3, ROWS, slots * SHELL), BF16),
            pltpu.VMEM((8, LANE), I32),
            pltpu.VMEM((2, chips, 8, LANE), I32),
            pltpu.SMEM((2, chips, 8, LANE), I32),
            pltpu.VMEM((2, slots + 1, slab, LANE), BF16),
            pltpu.VMEM((aux_rows, nu_w), BF16),
            pltpu.VMEM((aux_rows, nu_w), BF16),
            pltpu.VMEM((nvir, nu_w), BF16),
            pltpu.VMEM((n_occ, padded, nu_w), BF16),
            pltpu.VMEM((1, nvir), F32),
            pltpu.VMEM((n_occ, 1, -(-padded // LANE) * LANE), F32),
            pltpu.VMEM((padded, nu_w), BF16),
            pltpu.VMEM((padded, aux_rows), BF16),
            pltpu.VMEM((padded, nu_w), F32),
            pltpu.VMEM((n_occ, whole, nu_w), BF16),
            pltpu.VMEM((n_occ - 1, whole, nu_w), BF16),
            pltpu.VMEM((n_occ, ROWS, front), BF16),
            pltpu.VMEM((n_occ - 1, ROWS, front), BF16),
            pltpu.VMEM((padded, nu_w), BF16),
            pltpu.VMEM((farthest, padded, LANE), BF16),
            pltpu.VMEM((farthest, padded, LANE), BF16),
            pltpu.VMEM((farthest, padded - LANE, padded), BF16),
            pltpu.VMEM((farthest, padded - LANE, padded), BF16),
            pltpu.VMEM((farthest, padded, LANE), F32),
            pltpu.VMEM((farthest, padded - LANE, padded), F32),
            pltpu.VMEM((8, LANE), F32),
            pltpu.VMEM((n_occ, 8, LANE), F32),
            dma((chunks + 3,)),
            dma((chunks,)),
            dma((chips,)),
            dma((chips,)),
            dma((chunks, chips)),
            dma((chunks, chips)),
            dma((chips,)),
            dma((2, chips)),
            dma((chips,)),
            dma((chips,)),
            dma((len(pieces) + 1, n_occ - 1)),
            dma((len(pieces) + 1, n_occ - 1)),
            dma((farthest,)),
            dma((farthest,)),
            dma((farthest,)),
            dma((farthest,)),
            dma((n_occ,)),
            dma((n_occ,)),
        ],
        compiler_params=pltpu.CompilerParams(
            collective_id=0, has_side_effects=True, vmem_limit_bytes=60 * 2**20
        ),
        cost_estimate=pl.CostEstimate(flops=2 * macs, bytes_accessed=2 * nu_w * nvir, transcendentals=0),
    )(integrals, mu_shells, nu_shells, block_count, occ_t, vir_t, occ_order, occ_energies, vir_energies)


def local(
    n_aux,
    n_occ,
    integrals,
    mu_shells,
    nu_shells,
    block_count,
    occ_coeffs,
    vir_coeffs,
    occ_order,
    occ_energies,
    vir_energies,
):
    return pair_results(
        n_aux,
        n_occ,
        integrals[0],
        mu_shells,
        nu_shells,
        block_count,
        occ_coeffs.T,
        vir_coeffs.T,
        occ_order,
        occ_energies,
        vir_energies,
    )


def solution(mesh):
    placed = (
        P(("aux", "occ"), None, None, None),
        P(("aux", "occ"), None),
        P(("aux", "occ"), None),
        P(("aux", "occ")),
        P(),
        P(),
        P(),
        P(),
        P(),
    )
    return jax.shard_map(
        functools.partial(local, mesh.shape["aux"], mesh.shape["occ"]),
        mesh=mesh,
        in_specs=placed,
        out_specs=(P("aux", "occ", None), P("aux")),
        check_vma=False,
    )
```
